32 devices in a mesh: gx: 8 (over z, x), gy: 4 (over y, core).
Axes of the slice: x: 2, y: 2, z: 4, core: 2. Of those that a mesh axis runs over, the one named last changes fastest.
Arguments:
- innovations: bfloat16 [32, 64, 128], P(('gx', 'gy')), may hold values from -18 to 18
- station_columns: int32 [32, 128], P(('gx', 'gy')), may hold values from 0 to 8191
- profile_counts: int32 [32, 32], P(('gx', 'gy')), may hold values from 0 to 4, as said below
- land_mask: int32 [64, 4096], P('gy', 'gx'), may hold values 0 or 1
- vertical_coef: float32 [32, 64, 4096], P(None, 'gy', 'gx'), may hold values from 0.3 to 30
- inverse_x: bfloat16 [2, 4096, 4096], P(None, None, 'gx')
- inverse_y: bfloat16 [2, 64, 64], replicated
Outputs:
- increment: bfloat16 [64, 64, 4096], P(None, 'gy', 'gx')
- equivalents: bfloat16 [32, 64, 128], P(('gx', 'gy'))
The draws below stay inside these ranges and needn't reach their ends.
Inputs may be any that keep to these rules, and one draw needn't show every extreme that they name: `profile_counts`: every draw has one owner device that receives 4 live profiles from every device.
All inputs are finite; a program needn't handle non-finite values. No bound on the sum of `land_mask` on one device may be relied on, other than what follows from the above.
Results may differ from the reference program's by a relative error of at most 0.0061.
Values may be sent and summed in bfloat16 or wider, within the bound.
A program may use at most 64 MiB of HBM per device.

```python
import math
import jax
import jax.numpy as jnp

LEV = 32
CAP = 4
NX = 4096
CY = 16
CX = 512
LAYERS = 64
NY = 64
N_GX = 8
N_GY = 4
DEVICES = 32


def draw_profile_counts(key, part):
    key_hot = jax.random.fold_in(key, 11)
    key_cap = jax.random.fold_in(key, 12)
    key_base = jax.random.fold_in(key, 13)
    hot_owner = jax.random.randint(key_hot, (), 0, DEVICES)
    owner_cap = jax.random.randint(key_cap, (DEVICES,), 2, CAP + 1)
    base_draw = jax.random.randint(key_base, (DEVICES, DEVICES), 0, CAP + 1)
    limited = jnp.minimum(base_draw, owner_cap[None, :])
    owner_ids = jnp.arange(DEVICES, dtype=jnp.int32)[None, :]
    return jnp.where(owner_ids == hot_owner, CAP, limited).astype(jnp.int32)


def draw_inverse_x(key, part):
    key_scale = jax.random.fold_in(key, 21)
    key_factor = jax.random.fold_in(key, 22)
    positions = jnp.arange(NX, dtype=jnp.int32)
    distance = jnp.abs(positions[:, None] - positions[None, :])
    distance = jnp.minimum(distance, NX - distance).astype(jnp.float32)
    length_scale = jnp.exp(jax.random.uniform(key_scale, (2, 1, NX), jnp.float32, math.log(NX / 8.0), math.log(NX * 1.0)))
    factor = jax.random.uniform(key_factor, (2, NX, NX), jnp.float32, 0.5, 1.5)
    return (factor * jnp.exp(-distance[None, :, :] / length_scale) / jnp.sqrt(length_scale)).astype(jnp.bfloat16)


def draw_inverse_y(key, part):
    key_scale = jax.random.fold_in(key, 31)
    key_factor = jax.random.fold_in(key, 32)
    positions = jnp.arange(NY, dtype=jnp.int32)
    distance = jnp.abs(positions[:, None] - positions[None, :]).astype(jnp.float32)
    length_scale = jnp.exp(jax.random.uniform(key_scale, (2, 1, NY), jnp.float32, math.log(NY / 4.0), math.log(NY * 2.0)))
    factor = jax.random.uniform(key_factor, (2, NY, NY), jnp.float32, 0.5, 1.5)
    return (factor * jnp.exp(-distance[None, :, :] / length_scale) / jnp.sqrt(length_scale)).astype(jnp.bfloat16)


def place_ends(entries, own_key, least, largest):
    index_at = [jax.random.randint(jax.random.fold_in(own_key, axis), (), 0, length) for axis, length in enumerate(entries.shape)]
    main_axis = entries.shape.index(max(entries.shape))
    neighbour = index_at[:main_axis] + [(index_at[main_axis] + 1) % entries.shape[main_axis]] + index_at[main_axis + 1:]
    return entries.at[tuple(index_at)].set(least).at[tuple(neighbour)].set(largest)


def steps_of(own_key, extent, split, smallest, high):
    def one(dim, blocks):
        heights = jax.random.uniform(jax.random.fold_in(jax.random.fold_in(own_key, 6), dim), (blocks,), jnp.float32, smallest / len(split), high / len(split))
        return jnp.repeat(jnp.exp(heights), extent[dim] // blocks).reshape((-1,) + (1,) * (len(extent) - dim - 1))

    gain = one(*split[0])
    for cut in split[1:]:
        gain = gain * one(*cut)
    return gain


def normal_values(stream_key, dims, scale, reach, shards=(), held_as=jnp.bfloat16):
    values = jax.random.normal(stream_key, dims, jnp.float32) * scale
    if len(shards) > 0:
        values = steps_of(stream_key, dims, shards, -0.22, 0.18) * values
    return jnp.clip(values, min=-reach, max=reach).astype(held_as)


def setup_inputs(seed: int = 0) -> dict:
    seeds = jax.random.split(jax.random.key(seed), 8)
    return {
        "innovations": normal_values(seeds[0], (DEVICES, LAYERS, DEVICES * CAP), 3.0, 18.0, ((0, 32),)),
        "station_columns": place_ends(jax.random.randint(seeds[1], (DEVICES, DEVICES * CAP), 0, CY * CX), jax.random.fold_in(seeds[1], 1), 0, (CY * CX) - 1).astype(jnp.int32),
        "profile_counts": draw_profile_counts(jax.random.fold_in(seeds[7], 71), 0),
        "land_mask": place_ends((jax.random.randint(seeds[3], (NY, NX), 0, 4) < 3).astype(jnp.int32), jax.random.fold_in(seeds[3], 1), 0, 1),
        "vertical_coef": jnp.clip(jnp.exp(math.log(30.0) - 4.6051701 * jax.random.uniform(seeds[4], (LEV, NY, NX), jnp.float32) ** steps_of(seeds[4], (LEV, NY, NX), ((1, 4), (2, 8)), -0.2, 0.2)), 0.3, 30.0),
        "inverse_x": draw_inverse_x(jax.random.fold_in(seeds[7], 71), 0),
        "inverse_y": draw_inverse_y(jax.random.fold_in(seeds[7], 71), 0),
    }


def vertical_solve(rhs_field, coupling):
    levels = coupling.shape[0]
    zero_row = jnp.zeros_like(coupling[0])
    ratios = []
    partial_sol = []
    for level in range(levels):
        upper_coef = coupling[level + 1] if level + 1 < levels else zero_row
        diagonal = 1.0 + coupling[level] + upper_coef
        if level == 0:
            denominator = diagonal
            carried = rhs_field[:, 0]
        else:
            denominator = diagonal + coupling[level] * ratios[-1]
            carried = rhs_field[:, level] + coupling[level] * partial_sol[-1]
        ratios.append(-upper_coef / denominator)
        partial_sol.append(carried / denominator)
    solution = [partial_sol[-1]]
    for level in range(levels - 2, -1, -1):
        solution.append(partial_sol[level] - ratios[level] * solution[-1])
    return jnp.stack(solution[::-1], axis=1)


def reference(innovations, station_columns, profile_counts, land_mask, vertical_coef, inverse_x, inverse_y):
    devices_all = N_GX * N_GY
    layers = 2 * LEV
    slot_index = jnp.arange(CAP, dtype=jnp.int32)
    live = slot_index[None, None, :] < profile_counts[:, :, None]
    values = innovations.reshape(devices_all, layers, devices_all, CAP).astype(jnp.float32)
    values = jnp.where(live[:, None, :, :], values, jnp.zeros((), jnp.float32))
    owners = jnp.arange(devices_all, dtype=jnp.int32)
    owners_x = owners // N_GY
    owners_y = owners % N_GY
    local_cols = station_columns.reshape(devices_all, devices_all, CAP)
    global_index = (owners_y[:, None, None] * CY + local_cols // CX) * NX + owners_x[:, None, None] * CX + local_cols % CX
    flat_index = global_index.reshape(-1).astype(jnp.int32)
    ordered = jnp.transpose(values, (1, 2, 0, 3)).reshape(layers, devices_all * devices_all * CAP)
    gridded = jnp.zeros((layers, NY * NX), jnp.float32).at[:, flat_index].add(ordered)
    mask_field = land_mask.astype(jnp.float32).reshape(NY * NX)
    start_field = (gridded * mask_field).astype(jnp.bfloat16).reshape(2, LEV, NY, NX)
    results = []
    for tracer in range(2):
        along_x = jnp.dot(start_field[tracer].reshape(LEV * NY, NX), inverse_x[tracer], preferred_element_type=jnp.float32)
        along_x = along_x.astype(jnp.bfloat16).reshape(LEV, NY, NX)
        along_y = jnp.einsum("jm,kjc->kmc", inverse_y[tracer].astype(jnp.float32), along_x.astype(jnp.float32))
        results.append(along_y.astype(jnp.bfloat16))
    column_field = jnp.stack(results).astype(jnp.float32).reshape(2, LEV, NY * NX)
    solved = vertical_solve(column_field, vertical_coef.reshape(LEV, NY * NX))
    increment = (solved * mask_field[None, None, :]).astype(jnp.bfloat16).reshape(layers, NY, NX)
    picked = increment.reshape(layers, NY * NX)[:, flat_index].reshape(layers, devices_all, devices_all, CAP)
    picked = jnp.transpose(picked, (2, 0, 1, 3))
    equivalents = jnp.where(live[:, None, :, :], picked, jnp.zeros((), jnp.bfloat16))
    return increment, equivalents.reshape(devices_all, layers, devices_all * CAP)
```

```python
import functools
import jax
import jax.numpy as jnp
from jax import lax
from jax.experimental import pallas as pl
from jax.experimental.pallas import tpu as pltpu
from jax.sharding import PartitionSpec as P

LEV = 32
LANES = 128
TILE = 16
MESH = pl.DeviceIdType.MESH
F32 = jnp.float32
BF16 = jnp.bfloat16


def vertical_solve(rhs_field, coupling):
    levels = coupling.shape[0]
    zero_row = jnp.zeros_like(coupling[0])
    ratios = []
    partial_sol = []
    for level in range(levels):
        upper_coef = coupling[level + 1] if level + 1 < levels else zero_row
        diagonal = 1.0 + coupling[level] + upper_coef
        if level == 0:
            denominator = diagonal
            carried = rhs_field[:, 0]
        else:
            denominator = diagonal + coupling[level] * ratios[-1]
            carried = rhs_field[:, level] + coupling[level] * partial_sol[-1]
        ratios.append(-upper_coef / denominator)
        partial_sol.append(carried / denominator)
    solution = [partial_sol[-1]]
    for level in range(levels - 2, -1, -1):
        solution.append(partial_sol[level] - ratios[level] * solution[-1])
    return jnp.stack(solution[::-1], axis=1)


def body_exchange(
    innovations, station_columns, profile_counts, land_mask, vertical_coef, inverse_x, inverse_y
):
    layers = innovations.shape[1]
    devices_all = lax.axis_size(("gx", "gy"))
    devices_y = lax.axis_size("gy")
    capacity = innovations.shape[2] // devices_all
    slots = devices_all * capacity
    cells_y, cells_x = land_mask.shape
    cell_count = cells_y * cells_x
    tracers = inverse_x.shape[0]
    slot_index = lax.broadcasted_iota(jnp.int32, (devices_all, capacity), 1)
    live_flat = (slot_index < profile_counts[0][:, None]).reshape(slots)
    outgoing = jnp.where(live_flat[None, None, :], innovations, jnp.zeros((), jnp.bfloat16))
    arrived = lax.all_to_all(
        outgoing.reshape(layers, 1, devices_all, capacity),
        ("gx", "gy"),
        split_axis=2,
        concat_axis=1,
        tiled=True,
    )
    arrived = arrived.reshape(layers, slots)
    columns = station_columns[0]
    mask_flat = land_mask.reshape(cell_count)
    sea_slot = mask_flat[columns] > 0
    line_values = jnp.where(sea_slot[None, :], arrived, jnp.zeros((), jnp.bfloat16))
    line_columns = columns.reshape(1, slots)
    empty = jnp.zeros((tracers, layers // tracers, cells_y, cells_x), jnp.float32)
    values_piece = lax.all_gather(line_values, "gx", axis=1, tiled=True)
    columns_piece = lax.all_gather(line_columns, "gx", axis=1, tiled=True)
    sources = values_piece.shape[1] // slots

    def one_source(k, accum):
        block_values = lax.dynamic_slice_in_dim(values_piece, k * slots, slots, 1)
        block_columns = lax.dynamic_slice_in_dim(columns_piece, k * slots, slots, 1)[0]
        dense = (
            jnp.zeros((layers, cell_count), jnp.float32)
            .at[:, block_columns]
            .add(block_values.astype(jnp.float32))
        )
        dense = dense.astype(jnp.bfloat16).reshape(tracers, layers // tracers, cells_y, cells_x)
        source = k * slots // slots
        kernel_rows = lax.dynamic_slice_in_dim(inverse_x, source * cells_x, cells_x, 1)
        return accum + jnp.einsum(
            "tkjn,tnm->tkjm", dense, kernel_rows, preferred_element_type=jnp.float32
        )

    summed_x = lax.fori_loop(0, sources, one_source, empty)
    along_x = summed_x.astype(jnp.bfloat16).reshape(layers, cells_y, cells_x)
    rows_y = layers // devices_y
    tracer_y = lax.axis_index("gy") * rows_y // LEV
    matrix_y = lax.dynamic_index_in_dim(inverse_y, tracer_y, 0, keepdims=False)
    product = jnp.einsum(
        "rjc,jm->rmc",
        lax.all_to_all(along_x, "gy", split_axis=0, concat_axis=1, tiled=True),
        matrix_y,
        preferred_element_type=jnp.float32,
    ).astype(jnp.bfloat16)
    along_y = lax.all_to_all(product, "gy", split_axis=1, concat_axis=0, tiled=True)
    mask_field = mask_flat.astype(jnp.float32)
    column_field = along_y.astype(jnp.float32).reshape(2, LEV, cell_count)
    solved = vertical_solve(column_field, vertical_coef.reshape(LEV, cell_count))
    increment = (
        (solved * mask_field[None, None, :]).astype(jnp.bfloat16).reshape(layers, cells_y, cells_x)
    )
    picked = increment.reshape(layers, cell_count)[:, columns]
    returned = lax.all_to_all(
        picked.reshape(layers, 1, devices_all, capacity),
        ("gx", "gy"),
        split_axis=2,
        concat_axis=1,
        tiled=True,
    )
    returned = returned.reshape(1, layers, slots)
    equivalents = jnp.where(live_flat[None, None, :], returned, jnp.zeros((), jnp.bfloat16))
    return (increment, equivalents)


def iota(shape, dim):
    return lax.broadcasted_iota(jnp.int32, shape, dim)


def onehot(condition):
    return jnp.where(condition, 1.0, 0.0).astype(BF16)


def dot(a, b):
    return jnp.dot(a, b, preferred_element_type=F32)


def gather_kernel(
    dims, capacity, innov_ref, counts_ref, columns_ref, mask_ref, out_ref, mine, send_sem, recv_sem
):
    gx_outer, gx_inner, gy_outer, gy_inner = dims
    gx, gy = lax.axis_index("gx"), lax.axis_index("gy")
    i0, i1 = gx // gx_inner, lax.rem(gx, gx_inner)
    i2, i3 = gy // gy_inner, lax.rem(gy, gy_inner)
    far = [(lax.rem(i0 + k, gx_outer) * gx_inner + i1, gy) for k in range(1, gx_outer)]
    across = (i0 * gx_inner + (1 - i1), gy)
    along = (gx, (1 - i2) * gy_inner + i3)
    twin = (gx, i2 * gy_inner + (1 - i3))
    barrier = pltpu.get_barrier_semaphore()
    partners = far + [across, along, twin]
    for partner in partners:
        pl.semaphore_signal(barrier, inc=1, device_id=partner, device_id_type=MESH)

    layers, slots = innov_ref.shape
    devices = counts_ref.shape[1]
    cells_y, cells_x = mask_ref.shape
    counts = jnp.broadcast_to(counts_ref[...].astype(F32), (8, devices)).astype(BF16)
    lane_count = dot(
        counts, onehot(iota((devices, slots), 0) == iota((devices, slots), 1) // capacity)
    )[0:1]
    live = lax.rem(iota((1, slots), 1), capacity).astype(F32) < lane_count
    values = jnp.where(live, innov_ref[...].astype(F32), 0.0)
    half = slots // 2
    packed = jnp.concatenate([values, pltpu.roll(values, half, 1)], axis=0).T
    mine[0:half] = packed[0:half].astype(BF16)
    columns = columns_ref[...]
    cell_i = lax.rem(columns, cells_x)
    cell_j = columns // cells_x
    at_i = onehot(iota((cells_x, slots), 0) == cell_i)
    masks = dot(mask_ref[...].astype(F32).astype(BF16), at_i)
    sea = jnp.sum(jnp.where(iota((cells_y, slots), 0) == cell_j, masks, 0.0), 0, keepdims=True)
    kinds = [jnp.where(sea > 0.0, cell_i // 2, -cells_x), lax.rem(cell_i, 2), cell_j]
    per_row = LANES // TILE
    l_in = iota((slots, LANES), 0)
    l_out = iota((slots, LANES), 1)
    info = jnp.zeros((TILE, LANES), F32)
    in_row = iota((TILE, slots), 0) == iota((TILE, slots), 1) // (capacity * per_row)
    for kind, value in enumerate(kinds):
        spread = (
            (l_out // TILE == lax.rem(l_in // capacity, per_row))
            & (lax.rem(l_out, capacity) == lax.rem(l_in, capacity))
            & (lax.rem(l_out, TILE) // capacity == kind)
        )
        info += dot(jnp.where(in_row, value.astype(F32), 0.0).astype(BF16), onehot(spread))
    mine[half : half + TILE] = info.astype(BF16)
    out_ref[i0, i1, i2, i3] = mine[...]

    pl.semaphore_wait(barrier, len(partners))
    copies = []
    for k, partner in enumerate(far):
        copy = pltpu.make_async_remote_copy(
            src_ref=mine,
            dst_ref=out_ref.at[i0, i1, i2, i3],
            send_sem=send_sem.at[k],
            recv_sem=recv_sem.at[k],
            device_id=partner,
            device_id_type=MESH,
        )
        copy.start()
        copies.append(copy)
    for copy in copies:
        copy.wait_recv()
    stages = [
        (out_ref.at[:, i1, i2, i3], across),
        (out_ref.at[:, :, i2, i3], along),
        (out_ref.at[:, :, :, i3], twin),
    ]
    for k, (block, partner) in enumerate(stages):
        copy = pltpu.make_async_remote_copy(
            src_ref=block,
            dst_ref=block,
            send_sem=send_sem.at[len(far) + k],
            recv_sem=recv_sem.at[len(far) + k],
            device_id=partner,
            device_id_type=MESH,
        )
        copy.start()
        copy.wait_recv()
        copies.append(copy)
    for copy in copies:
        copy.wait_send()


def field_kernel(
    capacity,
    all_ref,
    kernel_x_ref,
    kernel_y_ref,
    coef_ref,
    mask_ref,
    columns_ref,
    inc_ref,
    picked_ref,
    acc,
    inverse,
    left,
    turned,
):
    block = pl.program_id(0)
    blocks = pl.num_programs(0)
    devices, _, _ = all_ref.shape
    tracers, cells_x, _ = kernel_x_ref.shape
    _, cells_y, rows_j = kernel_y_ref.shape
    levels = coef_ref.shape[0]
    layers = tracers * levels
    devices_y = devices // blocks
    per_block = devices_y * capacity
    profiles = devices * per_block
    per_row = LANES // TILE

    @pl.when(block == 0)
    def _():
        acc[...] = jnp.zeros_like(acc)
        ratio = None
        for k in range(levels):
            diagonal = 1.0 + coef_ref[k]
            if k + 1 < levels:
                diagonal += coef_ref[k + 1]
            if k > 0:
                diagonal += coef_ref[k] * ratio
            inv = 1.0 / diagonal
            inverse[k] = inv
            if k + 1 < levels:
                ratio = -coef_ref[k + 1] * inv

    shape = (profiles, devices_y * TILE)
    p, q = iota(shape, 0), iota(shape, 1)
    owner = lax.rem(p // capacity, devices_y)
    repeat = onehot(q == owner * TILE + p // (per_block * per_row))
    info = all_ref[pl.ds(block * devices_y, devices_y), layers : layers + TILE, :]
    info = dot(repeat, info.reshape(devices_y * TILE, LANES))
    shape = (profiles, LANES)
    p, q = iota(shape, 0), iota(shape, 1)
    own = (q // TILE == lax.rem(p // per_block, per_row)) & (
        lax.rem(q, capacity) == lax.rem(p, capacity)
    )
    info = jnp.where(own, info, 0.0).astype(BF16)
    shape = (LANES, cells_x + LANES)
    kind, n = lax.rem(iota(shape, 0), TILE) // capacity, iota(shape, 1)
    weight = jnp.where(
        n < cells_x,
        jnp.where(kind == 0, 2.0, jnp.where(kind == 1, 1.0, 0.0)),
        jnp.where(kind == 2, 1.0, 0.0),
    ).astype(BF16)
    place = dot(info, weight).astype(jnp.int32)
    at_i = onehot(place[:, :cells_x] == iota((profiles, cells_x), 1))
    p, q = iota((profiles, LANES), 0), iota((profiles, LANES), 1)
    at_j = onehot(place[:, cells_x:] + lax.rem(p // capacity, devices_y) * cells_y == q)[:, :rows_j]

    pieces = layers // per_block
    piece = lax.rem(block, pieces)
    part = all_ref[:, pl.ds(pl.multiple_of(piece * per_block, per_block), per_block), :]
    turned[...] = part.reshape(profiles, LANES).astype(F32).T
    values = turned[pl.ds(pl.multiple_of(block // pieces * layers, layers), layers), :]

    for t in range(tracers):
        smooth_y = lax.dot_general(
            kernel_y_ref[t], at_j, (((1,), (1,)), ((), ())), preferred_element_type=F32
        )
        for k in range(levels):
            r = t * levels + k
            left[t, k * cells_y : (k + 1) * cells_y, :] = (
                smooth_y * values[r : r + 1, :]
            ).astype(BF16)
        right = dot(at_i, kernel_x_ref[t]).astype(BF16)
        acc[t] += dot(left[t], right)

    @pl.when(block == blocks - 1)
    def _():
        mask = mask_ref[...].astype(F32)
        for t in range(tracers):
            carried = None
            for k in range(levels):
                rows = slice(k * cells_y, (k + 1) * cells_y)
                value = acc[t, rows, :]
                if k > 0:
                    value += coef_ref[k] * carried
                carried = value * inverse[k]
                acc[t, rows, :] = carried
            for k in range(levels - 1, -1, -1):
                if k + 1 < levels:
                    rows = slice(k * cells_y, (k + 1) * cells_y)
                    carried = acc[t, rows, :] + coef_ref[k + 1] * inverse[k] * carried
                inc_ref[t * levels + k] = (carried * mask).astype(BF16)
        columns = columns_ref[...]
        slots = columns.shape[1]
        at_own = onehot(iota((cells_x, slots), 0) == lax.rem(columns, cells_x))
        field = inc_ref[...].reshape(layers * cells_y, cells_x)
        found = dot(field, at_own).reshape(layers, cells_y, slots)
        in_row = iota((1, cells_y, slots), 1) == (columns // cells_x)[None]
        picked_ref[...] = jnp.sum(jnp.where(in_row, found, 0.0), axis=1)


def return_kernel(
    capacity, picked_ref, counts_ref, out_ref, outgoing, arrived, rows, send_sem, recv_sem
):
    gx, gy = lax.axis_index("gx"), lax.axis_index("gy")
    n_gy = lax.axis_size("gy")
    layers, slots = picked_ref.shape
    devices = counts_ref.shape[1]
    me = gx * n_gy + gy
    others = [lax.rem(me + k, devices) for k in range(1, devices)]
    places = [(other // n_gy, lax.rem(other, n_gy)) for other in others]
    barrier = pltpu.get_barrier_semaphore()
    for place in places:
        pl.semaphore_signal(barrier, inc=1, device_id=place, device_id_type=MESH)
    picked = picked_ref[...]
    turned = jnp.concatenate([picked, jnp.zeros((slots - layers, slots), F32)], axis=0).T
    for d in range(devices):
        outgoing[d] = turned[d * capacity : (d + 1) * capacity]
    arrived[me] = outgoing[me]
    pl.semaphore_wait(barrier, devices - 1)
    copies = []
    for k, (other, place) in enumerate(zip(others, places)):
        copy = pltpu.make_async_remote_copy(
            src_ref=outgoing.at[other],
            dst_ref=arrived.at[me],
            send_sem=send_sem.at[k],
            recv_sem=recv_sem.at[k],
            device_id=place,
            device_id_type=MESH,
        )
        copy.start()
        copies.append(copy)
    for copy in copies:
        copy.wait_recv()
    for d in range(devices):
        rows[d * capacity : (d + 1) * capacity] = arrived[d]
    counts = jnp.broadcast_to(counts_ref[...].astype(F32), (8, devices)).astype(BF16)
    lane_count = dot(
        counts, onehot(iota((devices, slots), 0) == iota((devices, slots), 1) // capacity)
    )[0:1]
    live = lax.rem(iota((1, slots), 1), capacity).astype(F32) < lane_count
    out_ref[...] = jnp.where(live, rows[...].T[:layers], 0.0).astype(BF16)
    for copy in copies:
        copy.wait_send()


def body_gather(
    dims,
    innovations,
    station_columns,
    profile_counts,
    land_mask,
    vertical_coef,
    inverse_x,
    inverse_y,
):
    layers, slots = innovations.shape[1:]
    devices = profile_counts.shape[1]
    devices_x, devices_y = lax.axis_size("gx"), lax.axis_size("gy")
    capacity = slots // devices
    cells_y, cells_x = land_mask.shape
    tracers = inverse_x.shape[0]
    levels = layers // tracers
    vmem = pl.BlockSpec(memory_space=pltpu.VMEM)
    n_copies = dims[0] - 1 + 3
    height = slots // 2 + TILE
    gathered = pl.pallas_call(
        functools.partial(gather_kernel, dims, capacity),
        out_shape=jax.ShapeDtypeStruct(dims + (height, LANES), BF16),
        in_specs=[vmem] * 4,
        out_specs=vmem,
        scratch_shapes=[
            pltpu.VMEM((height, LANES), BF16),
            pltpu.SemaphoreType.DMA((n_copies,)),
            pltpu.SemaphoreType.DMA((n_copies,)),
        ],
        compiler_params=pltpu.CompilerParams(
            collective_id=0, has_side_effects=True, vmem_limit_bytes=16 << 20
        ),
        name="gather_profiles",
    )(innovations[0], profile_counts, station_columns, land_mask)
    gathered = gathered.reshape(devices, height, LANES)
    own_y = lax.dynamic_slice_in_dim(inverse_y, lax.axis_index("gy") * cells_y, cells_y, 2)
    own_y = jnp.swapaxes(own_y, 1, 2)
    profiles = devices * devices_y * capacity
    rows = levels * cells_y

    def whole(*shape):
        return pl.BlockSpec(shape, lambda a: (0,) * len(shape))

    increment, picked = pl.pallas_call(
        functools.partial(field_kernel, capacity),
        grid=(devices_x,),
        out_shape=(
            jax.ShapeDtypeStruct((layers, cells_y, cells_x), BF16),
            jax.ShapeDtypeStruct((layers, slots), F32),
        ),
        in_specs=[
            whole(devices, height, LANES),
            pl.BlockSpec((tracers, cells_x, cells_x), lambda a: (0, a, 0)),
            whole(*own_y.shape),
            whole(levels, cells_y, cells_x),
            whole(cells_y, cells_x),
            whole(1, slots),
        ],
        out_specs=(whole(layers, cells_y, cells_x), whole(layers, slots)),
        scratch_shapes=[
            pltpu.VMEM((tracers, rows, cells_x), F32),
            pltpu.VMEM((levels, cells_y, cells_x), F32),
            pltpu.VMEM((tracers, rows, profiles), BF16),
            pltpu.VMEM((LANES, profiles), F32),
        ],
        compiler_params=pltpu.CompilerParams(vmem_limit_bytes=40 << 20),
        name="smooth_and_solve",
    )(gathered, inverse_x, own_y, vertical_coef, land_mask, station_columns)
    equivalents = pl.pallas_call(
        functools.partial(return_kernel, capacity),
        out_shape=jax.ShapeDtypeStruct((layers, slots), BF16),
        in_specs=[vmem] * 2,
        out_specs=vmem,
        scratch_shapes=[
            pltpu.VMEM((devices, capacity, LANES), F32),
            pltpu.VMEM((devices, capacity, LANES), F32),
            pltpu.VMEM((slots, LANES), F32),
            pltpu.SemaphoreType.DMA((devices - 1,)),
            pltpu.SemaphoreType.DMA((devices - 1,)),
        ],
        compiler_params=pltpu.CompilerParams(
            collective_id=1, has_side_effects=True, vmem_limit_bytes=16 << 20
        ),
        name="return_equivalents",
    )(picked, profile_counts)
    return increment, equivalents[None]


def plan(devices_x, devices_y, innovations, land_mask, inverse_x, inverse_y):
    devices = devices_x * devices_y
    layers, slots = innovations.shape[1:]
    capacity = slots // devices
    cells_x = land_mask.shape[1] // devices_x
    fits = (
        slots == LANES
        and 2 * layers == LANES
        and capacity * devices_y == TILE
        and 3 * capacity <= TILE
        and devices_x % 2 == 0
        and devices_y == 4
        and cells_x % LANES == 0
        and cells_x <= 512
        and inverse_y.shape[1] <= LANES
    )
    return (devices_x // 2, 2, devices_y // 2, 2) if fits else None


def solution(mesh):
    in_specs = (
        P(("gx", "gy"), None, None),
        P(("gx", "gy"), None),
        P(("gx", "gy"), None),
        P("gy", "gx"),
        P(None, "gy", "gx"),
        P(None, None, "gx"),
        P(),
    )
    out_specs = (P(None, "gy", "gx"), P(("gx", "gy"), None, None))

    def run(innovations, columns, counts, land_mask, coef, inverse_x, inverse_y):
        dims = plan(
            mesh.shape["gx"], mesh.shape["gy"], innovations, land_mask, inverse_x, inverse_y
        )
        body = body_exchange if dims is None else functools.partial(body_gather, dims)
        return jax.shard_map(
            body, mesh=mesh, in_specs=in_specs, out_specs=out_specs, check_vma=False
        )(innovations, columns, counts, land_mask, coef, inverse_x, inverse_y)

    return run
```

```python
import functools
import jax
import jax.numpy as jnp
from jax import lax
from jax.experimental import pallas as pl
from jax.experimental.pallas import tpu as pltpu
from jax.sharding import PartitionSpec as P

LEV = 32
LANES = 128
TILE = 16
VMEM_BYTES = 56 << 20
MESH = pl.DeviceIdType.MESH
F32 = jnp.float32
BF16 = jnp.bfloat16


def vertical_solve(rhs_field, coupling):
    levels = coupling.shape[0]
    zero_row = jnp.zeros_like(coupling[0])
    ratios = []
    partial_sol = []
    for level in range(levels):
        upper_coef = coupling[level + 1] if level + 1 < levels else zero_row
        diagonal = 1.0 + coupling[level] + upper_coef
        if level == 0:
            denominator = diagonal
            carried = rhs_field[:, 0]
        else:
            denominator = diagonal + coupling[level] * ratios[-1]
            carried = rhs_field[:, level] + coupling[level] * partial_sol[-1]
        ratios.append(-upper_coef / denominator)
        partial_sol.append(carried / denominator)
    solution = [partial_sol[-1]]
    for level in range(levels - 2, -1, -1):
        solution.append(partial_sol[level] - ratios[level] * solution[-1])
    return jnp.stack(solution[::-1], axis=1)


def body_exchange(
    innovations, station_columns, profile_counts, land_mask, vertical_coef, inverse_x, inverse_y
):
    layers = innovations.shape[1]
    devices_all = lax.axis_size(("gx", "gy"))
    devices_y = lax.axis_size("gy")
    capacity = innovations.shape[2] // devices_all
    slots = devices_all * capacity
    cells_y, cells_x = land_mask.shape
    cell_count = cells_y * cells_x
    tracers = inverse_x.shape[0]
    slot_index = lax.broadcasted_iota(jnp.int32, (devices_all, capacity), 1)
    live_flat = (slot_index < profile_counts[0][:, None]).reshape(slots)
    outgoing = jnp.where(live_flat[None, None, :], innovations, jnp.zeros((), jnp.bfloat16))
    arrived = lax.all_to_all(
        outgoing.reshape(layers, 1, devices_all, capacity),
        ("gx", "gy"),
        split_axis=2,
        concat_axis=1,
        tiled=True,
    )
    arrived = arrived.reshape(layers, slots)
    columns = station_columns[0]
    mask_flat = land_mask.reshape(cell_count)
    sea_slot = mask_flat[columns] > 0
    line_values = jnp.where(sea_slot[None, :], arrived, jnp.zeros((), jnp.bfloat16))
    line_columns = columns.reshape(1, slots)
    empty = jnp.zeros((tracers, layers // tracers, cells_y, cells_x), jnp.float32)
    values_piece = lax.all_gather(line_values, "gx", axis=1, tiled=True)
    columns_piece = lax.all_gather(line_columns, "gx", axis=1, tiled=True)
    sources = values_piece.shape[1] // slots

    def one_source(k, accum):
        block_values = lax.dynamic_slice_in_dim(values_piece, k * slots, slots, 1)
        block_columns = lax.dynamic_slice_in_dim(columns_piece, k * slots, slots, 1)[0]
        dense = (
            jnp.zeros((layers, cell_count), jnp.float32)
            .at[:, block_columns]
            .add(block_values.astype(jnp.float32))
        )
        dense = dense.astype(jnp.bfloat16).reshape(tracers, layers // tracers, cells_y, cells_x)
        source = k * slots // slots
        kernel_rows = lax.dynamic_slice_in_dim(inverse_x, source * cells_x, cells_x, 1)
        return accum + jnp.einsum(
            "tkjn,tnm->tkjm", dense, kernel_rows, preferred_element_type=jnp.float32
        )

    summed_x = lax.fori_loop(0, sources, one_source, empty)
    along_x = summed_x.astype(jnp.bfloat16).reshape(layers, cells_y, cells_x)
    rows_y = layers // devices_y
    tracer_y = lax.axis_index("gy") * rows_y // LEV
    matrix_y = lax.dynamic_index_in_dim(inverse_y, tracer_y, 0, keepdims=False)
    product = jnp.einsum(
        "rjc,jm->rmc",
        lax.all_to_all(along_x, "gy", split_axis=0, concat_axis=1, tiled=True),
        matrix_y,
        preferred_element_type=jnp.float32,
    ).astype(jnp.bfloat16)
    along_y = lax.all_to_all(product, "gy", split_axis=1, concat_axis=0, tiled=True)
    mask_field = mask_flat.astype(jnp.float32)
    column_field = along_y.astype(jnp.float32).reshape(2, LEV, cell_count)
    solved = vertical_solve(column_field, vertical_coef.reshape(LEV, cell_count))
    increment = (
        (solved * mask_field[None, None, :]).astype(jnp.bfloat16).reshape(layers, cells_y, cells_x)
    )
    picked = increment.reshape(layers, cell_count)[:, columns]
    returned = lax.all_to_all(
        picked.reshape(layers, 1, devices_all, capacity),
        ("gx", "gy"),
        split_axis=2,
        concat_axis=1,
        tiled=True,
    )
    returned = returned.reshape(1, layers, slots)
    equivalents = jnp.where(live_flat[None, None, :], returned, jnp.zeros((), jnp.bfloat16))
    return (increment, equivalents)


def iota(shape, dim):
    return lax.broadcasted_iota(jnp.int32, shape, dim)


def onehot(condition):
    return jnp.where(condition, 1.0, 0.0).astype(BF16)


def dot(a, b):
    return jnp.dot(a, b, preferred_element_type=F32)


def profile_kernel(
    dims,
    capacity,
    innov_hbm,
    columns_hbm,
    counts_hbm,
    mask_hbm,
    coef_hbm,
    kernel_x_hbm,
    kernel_y_hbm,
    inc_hbm,
    equiv_hbm,
    innov_ref,
    columns_ref,
    counts_ref,
    mask_ref,
    coef_ref,
    kernel_x_ref,
    kernel_y_ref,
    cells,
    profiles,
    smooth_y,
    left,
    turned,
    acc,
    inverse,
    ratio,
    inc_ref,
    outgoing,
    arrived,
    rows,
    equiv_ref,
    load_sem,
    store_sem,
    cell_send,
    cell_recv,
    prof_send,
    prof_recv,
    back_send,
    back_recv,
):
    gx_outer, gx_inner, gy_outer, gy_inner = dims
    blocks, devices_y = gx_outer * gx_inner, gy_outer * gy_inner
    gx, gy = lax.axis_index("gx"), lax.axis_index("gy")
    i0, i1 = gx // gx_inner, lax.rem(gx, gx_inner)
    i2, i3 = gy // gy_inner, lax.rem(gy, gy_inner)
    me = gx * devices_y + gy
    layers, slots = innov_ref.shape
    devices = blocks * devices_y
    levels, cells_y, cells_x = coef_ref.shape
    tracers, rows_j, _ = kernel_y_ref.shape
    per_block = devices_y * capacity
    count = devices * per_block

    loads = [
        pltpu.make_async_copy(source, target, load_sem.at[k])
        for k, (source, target) in enumerate(
            [
                (columns_hbm, columns_ref),
                (mask_hbm, mask_ref),
                (counts_hbm, counts_ref),
                (innov_hbm, innov_ref),
                (coef_hbm, coef_ref),
                (kernel_y_hbm, kernel_y_ref),
                (kernel_x_hbm, kernel_x_ref),
            ]
        )
    ]
    for load in loads:
        load.start()

    def place(k):
        other = lax.rem(me + k, devices)
        return other, (other // devices_y, lax.rem(other, devices_y))

    barrier = pltpu.get_barrier_semaphore()

    @pl.loop(1, devices)
    def _(k):
        pl.semaphore_signal(barrier, inc=1, device_id=place(k)[1], device_id_type=MESH)

    loads[0].wait()
    loads[1].wait()
    columns = columns_ref[...]
    cell_i, cell_j = columns & (cells_x - 1), columns // cells_x
    at_own = onehot(iota((cells_x, slots), 0) == cell_i)
    masks = dot(mask_ref[...].astype(F32).astype(BF16), at_own)
    sea = jnp.sum(jnp.where(iota((cells_y, slots), 0) == cell_j, masks, 0.0), 0, keepdims=True)
    cells[me] = jnp.where(sea > 0.0, columns, -1)
    pl.semaphore_wait(barrier, devices - 1)

    def cell_copy(k):
        return pltpu.make_async_remote_copy(
            src_ref=cells.at[me],
            dst_ref=cells.at[me],
            send_sem=cell_send.at[k - 1],
            recv_sem=cell_recv.at[k - 1],
            device_id=place(k)[1],
            device_id_type=MESH,
        )

    @pl.loop(1, devices)
    def _(k):
        cell_copy(k).start()

    loads[2].wait()
    loads[3].wait()
    counts = jnp.broadcast_to(counts_ref[...].astype(F32), (8, devices)).astype(BF16)
    lane_count = dot(
        counts, onehot(iota((devices, slots), 0) == iota((devices, slots), 1) // capacity)
    )[0:1]
    live = (iota((1, slots), 1) & (capacity - 1)).astype(F32) < lane_count
    values = jnp.where(live, innov_ref[...].astype(F32), 0.0)
    half = slots // 2
    packed = jnp.concatenate([values, pltpu.roll(values, half, 1)], axis=0).T
    profiles[i0, i1, i2, i3] = packed[0:half].astype(BF16)

    sent = []

    def send(block, partner):
        copy = pltpu.make_async_remote_copy(
            src_ref=block,
            dst_ref=block,
            send_sem=prof_send.at[len(sent)],
            recv_sem=prof_recv.at[len(sent)],
            device_id=partner,
            device_id_type=MESH,
        )
        copy.start()
        sent.append(copy)
        return copy

    across = (i0 * gx_inner + (1 - i1), gy)
    along = (gx, (1 - i2) * gy_inner + i3)
    twin = (gx, i2 * gy_inner + (1 - i3))
    far = [
        send(
            profiles.at[i0, i1, i2, i3],
            (lax.rem(i0 + k, gx_outer) * gx_inner + i1, gy),
        )
        for k in range(1, gx_outer)
    ]

    loads[4].wait()
    last = None
    for k in range(levels):
        diagonal = 1.0 + coef_ref[k]
        if k + 1 < levels:
            diagonal += coef_ref[k + 1]
        if k > 0:
            diagonal -= coef_ref[k] * last
        inv = 1.0 / diagonal
        inverse[k] = inv
        if k + 1 < levels:
            last = coef_ref[k + 1] * inv
            ratio[k] = last

    for copy in far:
        copy.wait_recv()
    own_line = profiles.at[:, i1, i2, i3]
    by_x = send(own_line, across)
    by_y = send(own_line, along)
    to_twin = [send(own_line, twin)]

    @pl.loop(1, devices)
    def _(k):
        cell_copy(k).wait_recv()

    loads[5].wait()
    loads[6].wait()
    own_rows = onehot(iota((cells_y, rows_j), 1) == gy * cells_y + iota((cells_y, rows_j), 0))
    own_y = [
        lax.dot_general(
            own_rows, kernel_y_ref[t], (((1,), (1,)), ((), ())), preferred_element_type=F32
        ).astype(BF16)
        for t in range(tracers)
    ]
    row = iota((per_block, slots), 0)
    shape = (devices, per_block, slots)
    own_lane = iota(shape, 2) == iota(shape, 0) * capacity + (iota(shape, 1) & (capacity - 1))
    own_lane = jnp.where(own_lane, 1.0, 0.0)
    owner = (iota((count, 1), 0) & (per_block - 1)) // capacity

    def pick_rows(block):
        tile = jnp.zeros((per_block, slots), jnp.int32)
        for b in range(devices_y):
            tile = jnp.where(row // capacity == b, cells[block * devices_y + b], tile)
        cell = jnp.sum(own_lane * tile.astype(F32)[None], axis=2, keepdims=True)
        cell = cell.reshape(count, 1).astype(jnp.int32)
        column = jnp.where(cell < 0, -1, cell & (cells_x - 1))
        at_i = onehot(iota((count, cells_x), 1) == column)
        at_j = onehot(iota((count, rows_j), 1) == owner * cells_y + (cell // cells_x))
        lines = pl.ds(pl.multiple_of(block * cells_x, cells_x), cells_x)
        for t in range(tracers):
            smooth_y[block, t] = lax.dot_general(
                own_y[t], at_j, (((1,), (1,)), ((), ())), preferred_element_type=F32
            )
            kernel_x_ref[t, lines, :] = dot(at_i, kernel_x_ref[t, lines, :]).astype(BF16)

    pl.loop(0, blocks // 4)(pick_rows)
    by_x.wait_recv()
    by_y.wait_recv()
    from_x, from_y = profiles.at[:, 1 - i1, i2, i3], profiles.at[:, i1, 1 - i2, i3]
    diagonals = [
        send(from_x.at[:, 0 : half // 2], along),
        send(from_y.at[:, half // 2 : half], across),
    ]
    to_twin += [send(from_x, twin), send(from_y, twin)]
    pl.loop(blocks // 4, blocks // 2)(pick_rows)
    for copy in diagonals:
        copy.wait_recv()
    to_twin.append(send(profiles.at[:, 1 - i1, 1 - i2, i3], twin))
    pl.loop(blocks // 2, blocks)(pick_rows)
    for copy in to_twin:
        copy.wait_recv()

    pieces = half // per_block
    acc[...] = jnp.zeros_like(acc)

    @pl.loop(0, blocks)
    def _(block):
        piece = pl.multiple_of(lax.rem(block, pieces) * per_block, per_block)
        part = profiles[:, :, :, :, pl.ds(piece, per_block), :]
        turned[...] = part.reshape(count, LANES).astype(F32).T
        base = pl.multiple_of(block // pieces * layers, layers)
        values = turned[pl.ds(base, layers), :]
        lines = pl.ds(pl.multiple_of(block * cells_x, cells_x), cells_x)
        for t in range(tracers):
            weights = smooth_y[block, t]
            for k in range(levels):
                r = t * levels + k
                left[t, k * cells_y : (k + 1) * cells_y, :] = (
                    weights * values[r : r + 1, :]
                ).astype(BF16)
            acc[t] += dot(left[t], kernel_x_ref[t, lines, :])

    mask = mask_ref[...].astype(F32)
    carried = [None] * tracers
    for k in range(levels):
        lines = slice(k * cells_y, (k + 1) * cells_y)
        for t in range(tracers):
            value = acc[t, lines, :]
            if k > 0:
                value += coef_ref[k] * carried[t]
            carried[t] = value * inverse[k]
            acc[t, lines, :] = carried[t]
    for k in range(levels - 1, -1, -1):
        lines = slice(k * cells_y, (k + 1) * cells_y)
        for t in range(tracers):
            if k + 1 < levels:
                carried[t] = acc[t, lines, :] + ratio[k] * carried[t]
            inc_ref[t * levels + k] = (carried[t] * mask).astype(BF16)
    store = pltpu.make_async_copy(inc_ref, inc_hbm, store_sem.at[0])
    store.start()

    field = inc_ref[...].reshape(layers * cells_y, cells_x)
    found = dot(field, at_own).reshape(layers, cells_y, slots)
    in_row = iota((1, cells_y, slots), 1) == cell_j[None]
    picked = jnp.sum(jnp.where(in_row, found, 0.0), axis=1)
    picked = jnp.concatenate([picked, jnp.zeros((slots - layers, slots), F32)], axis=0).T
    for d in range(devices):
        outgoing[d] = picked[d * capacity : (d + 1) * capacity]
    arrived[me] = outgoing[me]

    def back_copy(k):
        other, where = place(k)
        return pltpu.make_async_remote_copy(
            src_ref=outgoing.at[other],
            dst_ref=arrived.at[me],
            send_sem=back_send.at[k - 1],
            recv_sem=back_recv.at[k - 1],
            device_id=where,
            device_id_type=MESH,
        )

    @pl.loop(1, devices)
    def _(k):
        back_copy(k).start()

    for copy in sent:
        copy.wait_send()

    @pl.loop(1, devices)
    def _(k):
        cell_copy(k).wait_send()

    @pl.loop(1, devices)
    def _(k):
        back_copy(k).wait_recv()

    for d in range(devices):
        rows[d * capacity : (d + 1) * capacity] = arrived[d]
    equiv_ref[...] = jnp.where(live, rows[...].T[:layers], 0.0).astype(BF16)
    result = pltpu.make_async_copy(equiv_ref, equiv_hbm, store_sem.at[1])
    result.start()

    @pl.loop(1, devices)
    def _(k):
        back_copy(k).wait_send()

    store.wait()
    result.wait()


def body_gather(
    dims,
    innovations,
    station_columns,
    profile_counts,
    land_mask,
    vertical_coef,
    inverse_x,
    inverse_y,
):
    layers, slots = innovations.shape[1:]
    devices = profile_counts.shape[1]
    devices_y = dims[2] * dims[3]
    capacity = slots // devices
    cells_y, cells_x = land_mask.shape
    tracers = inverse_x.shape[0]
    levels = layers // tracers
    blocks = dims[0] * dims[1]
    count = devices * devices_y * capacity
    anywhere = pl.BlockSpec(memory_space=pl.ANY)
    operands = (
        innovations[0],
        station_columns,
        profile_counts,
        land_mask,
        vertical_coef,
        inverse_x,
        inverse_y,
    )
    n_profile = dims[0] - 1 + 8
    increment, equivalents = pl.pallas_call(
        functools.partial(profile_kernel, dims, capacity),
        out_shape=(
            jax.ShapeDtypeStruct((layers, cells_y, cells_x), BF16),
            jax.ShapeDtypeStruct((layers, slots), BF16),
        ),
        in_specs=[anywhere] * len(operands),
        out_specs=(anywhere, anywhere),
        scratch_shapes=[pltpu.VMEM(x.shape, x.dtype) for x in operands]
        + [
            pltpu.VMEM((devices, 1, slots), jnp.int32),
            pltpu.VMEM(dims + (slots // 2, LANES), BF16),
            pltpu.VMEM((blocks, tracers, cells_y, count), F32),
            pltpu.VMEM((tracers, levels * cells_y, count), BF16),
            pltpu.VMEM((LANES, count), F32),
            pltpu.VMEM((tracers, levels * cells_y, cells_x), F32),
            pltpu.VMEM((levels, cells_y, cells_x), F32),
            pltpu.VMEM((levels, cells_y, cells_x), F32),
            pltpu.VMEM((layers, cells_y, cells_x), BF16),
            pltpu.VMEM((devices, capacity, LANES), F32),
            pltpu.VMEM((devices, capacity, LANES), F32),
            pltpu.VMEM((slots, LANES), F32),
            pltpu.VMEM((layers, slots), BF16),
            pltpu.SemaphoreType.DMA((len(operands),)),
            pltpu.SemaphoreType.DMA((2,)),
            pltpu.SemaphoreType.DMA((devices - 1,)),
            pltpu.SemaphoreType.DMA((devices - 1,)),
            pltpu.SemaphoreType.DMA((n_profile,)),
            pltpu.SemaphoreType.DMA((n_profile,)),
            pltpu.SemaphoreType.DMA((devices - 1,)),
            pltpu.SemaphoreType.DMA((devices - 1,)),
        ],
        compiler_params=pltpu.CompilerParams(
            collective_id=0, has_side_effects=True, vmem_limit_bytes=VMEM_BYTES
        ),
        name="smooth_profiles",
    )(*operands)
    return increment, equivalents[None]


def plan(devices_x, devices_y, innovations, land_mask, inverse_x, inverse_y):
    devices = devices_x * devices_y
    layers, slots = innovations.shape[1:]
    capacity = slots // devices
    cells_x = land_mask.shape[1] // devices_x
    fits = (
        slots == LANES
        and 2 * layers == LANES
        and capacity * devices_y == TILE
        and devices_x % 2 == 0
        and devices_y == 4
        and devices_x % 4 == 0
        and cells_x % LANES == 0
        and cells_x & (cells_x - 1) == 0
        and cells_x == devices * TILE
        and inverse_y.shape[1] <= LANES
    )
    return (devices_x // 2, 2, devices_y // 2, 2) if fits else None


def solution(mesh):
    in_specs = (
        P(("gx", "gy"), None, None),
        P(("gx", "gy"), None),
        P(("gx", "gy"), None),
        P("gy", "gx"),
        P(None, "gy", "gx"),
        P(None, None, "gx"),
        P(),
    )
    out_specs = (P(None, "gy", "gx"), P(("gx", "gy"), None, None))

    def run(innovations, columns, counts, land_mask, coef, inverse_x, inverse_y):
        dims = plan(
            mesh.shape["gx"], mesh.shape["gy"], innovations, land_mask, inverse_x, inverse_y
        )
        body = body_exchange if dims is None else functools.partial(body_gather, dims)
        return jax.shard_map(
            body, mesh=mesh, in_specs=in_specs, out_specs=out_specs, check_vma=False
        )(innovations, columns, counts, land_mask, coef, inverse_x, inverse_y)

    return run
```

```python
import functools
import jax
import jax.numpy as jnp
from jax import lax
from jax.experimental import pallas as pl
from jax.experimental.pallas import tpu as pltpu
from jax.sharding import PartitionSpec as P

LEV = 32
LANES = 128
TILE = 16
VMEM_BYTES = 56 << 20
MESH = pl.DeviceIdType.MESH
F32 = jnp.float32
BF16 = jnp.bfloat16


def vertical_solve(rhs_field, coupling):
    levels = coupling.shape[0]
    zero_row = jnp.zeros_like(coupling[0])
    ratios = []
    partial_sol = []
    for level in range(levels):
        upper_coef = coupling[level + 1] if level + 1 < levels else zero_row
        diagonal = 1.0 + coupling[level] + upper_coef
        if level == 0:
            denominator = diagonal
            carried = rhs_field[:, 0]
        else:
            denominator = diagonal + coupling[level] * ratios[-1]
            carried = rhs_field[:, level] + coupling[level] * partial_sol[-1]
        ratios.append(-upper_coef / denominator)
        partial_sol.append(carried / denominator)
    solution = [partial_sol[-1]]
    for level in range(levels - 2, -1, -1):
        solution.append(partial_sol[level] - ratios[level] * solution[-1])
    return jnp.stack(solution[::-1], axis=1)


def body_exchange(
    innovations, station_columns, profile_counts, land_mask, vertical_coef, inverse_x, inverse_y
):
    layers = innovations.shape[1]
    devices_all = lax.axis_size(("gx", "gy"))
    devices_y = lax.axis_size("gy")
    capacity = innovations.shape[2] // devices_all
    slots = devices_all * capacity
    cells_y, cells_x = land_mask.shape
    cell_count = cells_y * cells_x
    tracers = inverse_x.shape[0]
    slot_index = lax.broadcasted_iota(jnp.int32, (devices_all, capacity), 1)
    live_flat = (slot_index < profile_counts[0][:, None]).reshape(slots)
    outgoing = jnp.where(live_flat[None, None, :], innovations, jnp.zeros((), jnp.bfloat16))
    arrived = lax.all_to_all(
        outgoing.reshape(layers, 1, devices_all, capacity),
        ("gx", "gy"),
        split_axis=2,
        concat_axis=1,
        tiled=True,
    )
    arrived = arrived.reshape(layers, slots)
    columns = station_columns[0]
    mask_flat = land_mask.reshape(cell_count)
    sea_slot = mask_flat[columns] > 0
    line_values = jnp.where(sea_slot[None, :], arrived, jnp.zeros((), jnp.bfloat16))
    line_columns = columns.reshape(1, slots)
    empty = jnp.zeros((tracers, layers // tracers, cells_y, cells_x), jnp.float32)
    values_piece = lax.all_gather(line_values, "gx", axis=1, tiled=True)
    columns_piece = lax.all_gather(line_columns, "gx", axis=1, tiled=True)
    sources = values_piece.shape[1] // slots

    def one_source(k, accum):
        block_values = lax.dynamic_slice_in_dim(values_piece, k * slots, slots, 1)
        block_columns = lax.dynamic_slice_in_dim(columns_piece, k * slots, slots, 1)[0]
        dense = (
            jnp.zeros((layers, cell_count), jnp.float32)
            .at[:, block_columns]
            .add(block_values.astype(jnp.float32))
        )
        dense = dense.astype(jnp.bfloat16).reshape(tracers, layers // tracers, cells_y, cells_x)
        source = k * slots // slots
        kernel_rows = lax.dynamic_slice_in_dim(inverse_x, source * cells_x, cells_x, 1)
        return accum + jnp.einsum(
            "tkjn,tnm->tkjm", dense, kernel_rows, preferred_element_type=jnp.float32
        )

    summed_x = lax.fori_loop(0, sources, one_source, empty)
    along_x = summed_x.astype(jnp.bfloat16).reshape(layers, cells_y, cells_x)
    rows_y = layers // devices_y
    tracer_y = lax.axis_index("gy") * rows_y // LEV
    matrix_y = lax.dynamic_index_in_dim(inverse_y, tracer_y, 0, keepdims=False)
    product = jnp.einsum(
        "rjc,jm->rmc",
        lax.all_to_all(along_x, "gy", split_axis=0, concat_axis=1, tiled=True),
        matrix_y,
        preferred_element_type=jnp.float32,
    ).astype(jnp.bfloat16)
    along_y = lax.all_to_all(product, "gy", split_axis=1, concat_axis=0, tiled=True)
    mask_field = mask_flat.astype(jnp.float32)
    column_field = along_y.astype(jnp.float32).reshape(2, LEV, cell_count)
    solved = vertical_solve(column_field, vertical_coef.reshape(LEV, cell_count))
    increment = (
        (solved * mask_field[None, None, :]).astype(jnp.bfloat16).reshape(layers, cells_y, cells_x)
    )
    picked = increment.reshape(layers, cell_count)[:, columns]
    returned = lax.all_to_all(
        picked.reshape(layers, 1, devices_all, capacity),
        ("gx", "gy"),
        split_axis=2,
        concat_axis=1,
        tiled=True,
    )
    returned = returned.reshape(1, layers, slots)
    equivalents = jnp.where(live_flat[None, None, :], returned, jnp.zeros((), jnp.bfloat16))
    return (increment, equivalents)


def iota(shape, dim):
    return lax.broadcasted_iota(jnp.int32, shape, dim)


def onehot(condition):
    return jnp.where(condition, 1.0, 0.0).astype(BF16)


def dot(a, b):
    return jnp.dot(a, b, preferred_element_type=F32)


def profile_kernel(
    dims,
    capacity,
    innov_hbm,
    columns_hbm,
    counts_hbm,
    mask_hbm,
    coef_hbm,
    kernel_x_hbm,
    kernel_y_hbm,
    inc_hbm,
    equiv_hbm,
    innov_ref,
    columns_ref,
    counts_ref,
    mask_ref,
    coef_ref,
    kernel_x_ref,
    kernel_y_ref,
    cells,
    profiles,
    place_x,
    picked_x,
    smooth_y,
    left,
    turned,
    acc,
    inverse,
    ratio,
    inc_ref,
    outgoing,
    arrived,
    rows,
    equiv_ref,
    load_sem,
    store_sem,
    cell_send,
    cell_recv,
    prof_send,
    prof_recv,
    back_send,
    back_recv,
):
    gx_outer, gx_inner, gy_outer, gy_inner = dims
    blocks, devices_y = gx_outer * gx_inner, gy_outer * gy_inner
    gx, gy = lax.axis_index("gx"), lax.axis_index("gy")
    i0, i1 = gx // gx_inner, lax.rem(gx, gx_inner)
    i2, i3 = gy // gy_inner, lax.rem(gy, gy_inner)
    me = gx * devices_y + gy
    layers, slots = innov_ref.shape
    devices = blocks * devices_y
    levels, cells_y, cells_x = coef_ref.shape
    tracers, rows_j, _ = kernel_y_ref.shape
    per_block = devices_y * capacity
    count = devices * per_block

    loads = [
        pltpu.make_async_copy(source, target, load_sem.at[k])
        for k, (source, target) in enumerate(
            [
                (columns_hbm, columns_ref),
                (mask_hbm, mask_ref),
                (counts_hbm, counts_ref),
                (innov_hbm, innov_ref),
                (coef_hbm, coef_ref),
                (kernel_y_hbm, kernel_y_ref),
                (kernel_x_hbm, kernel_x_ref),
            ]
        )
    ]
    for load in loads:
        load.start()

    def place(k):
        other = lax.rem(me + k, devices)
        return other, (lax.div(other, devices_y), lax.rem(other, devices_y))

    barrier = pltpu.get_barrier_semaphore()

    @pl.loop(1, devices)
    def _(k):
        pl.semaphore_signal(barrier, inc=1, device_id=place(k)[1], device_id_type=MESH)

    loads[0].wait()
    loads[1].wait()
    columns = columns_ref[...]
    cell_i, cell_j = columns & (cells_x - 1), columns // cells_x
    at_own = onehot(iota((cells_x, slots), 0) == cell_i)
    masks = dot(mask_ref[...].astype(F32).astype(BF16), at_own)
    sea = jnp.sum(jnp.where(iota((cells_y, slots), 0) == cell_j, masks, 0.0), 0, keepdims=True)
    cells[me] = jnp.where(sea > 0.0, columns, -1)
    pl.semaphore_wait(barrier, devices - 1)

    def cell_copy(k):
        return pltpu.make_async_remote_copy(
            src_ref=cells.at[me],
            dst_ref=cells.at[me],
            send_sem=cell_send.at[k - 1],
            recv_sem=cell_recv.at[k - 1],
            device_id=place(k)[1],
            device_id_type=MESH,
        )

    @pl.loop(1, devices)
    def _(k):
        cell_copy(k).start()

    loads[2].wait()
    loads[3].wait()
    counts = jnp.broadcast_to(counts_ref[...].astype(F32), (8, devices)).astype(BF16)
    lane_count = dot(
        counts, onehot(iota((devices, slots), 0) == iota((devices, slots), 1) // capacity)
    )[0:1]
    live = (iota((1, slots), 1) & (capacity - 1)).astype(F32) < lane_count
    values = jnp.where(live, innov_ref[...].astype(F32), 0.0)
    half = slots // 2
    packed = jnp.concatenate([values, pltpu.roll(values, half, 1)], axis=0).T
    profiles[i0, i1, i2, i3] = packed[0:half].astype(BF16)

    sent = []

    def send(block, partner):
        copy = pltpu.make_async_remote_copy(
            src_ref=block,
            dst_ref=block,
            send_sem=prof_send.at[len(sent)],
            recv_sem=prof_recv.at[len(sent)],
            device_id=partner,
            device_id_type=MESH,
        )
        copy.start()
        sent.append(copy)
        return copy

    across = (i0 * gx_inner + (1 - i1), gy)
    along = (gx, (1 - i2) * gy_inner + i3)
    twin = (gx, i2 * gy_inner + (1 - i3))
    far = [
        send(
            profiles.at[i0, i1, i2, i3],
            (lax.rem(i0 + k, gx_outer) * gx_inner + i1, gy),
        )
        for k in range(1, gx_outer)
    ]

    loads[4].wait()
    last = None
    for k in range(levels):
        diagonal = 1.0 + coef_ref[k]
        if k + 1 < levels:
            diagonal += coef_ref[k + 1]
        if k > 0:
            diagonal -= coef_ref[k] * last
        inv = 1.0 / diagonal
        inverse[k] = inv
        if k + 1 < levels:
            last = coef_ref[k + 1] * inv
            ratio[k] = last

    for copy in far:
        copy.wait_recv()
    own_line = profiles.at[:, i1, i2, i3]
    by_x = send(own_line, across)
    by_y = send(own_line, along)
    to_twin = [send(own_line, twin)]

    @pl.loop(1, devices)
    def _(k):
        cell_copy(k).wait_recv()

    loads[5].wait()
    loads[6].wait()
    own_rows = onehot(iota((cells_y, rows_j), 1) == gy * cells_y + iota((cells_y, rows_j), 0))
    own_y = [
        lax.dot_general(
            own_rows, kernel_y_ref[t], (((1,), (1,)), ((), ())), preferred_element_type=F32
        ).astype(BF16)
        for t in range(tracers)
    ]
    row = iota((per_block, slots), 0)
    shape = (devices, per_block, slots)
    own_lane = iota(shape, 2) == iota(shape, 0) * capacity + (iota(shape, 1) & (capacity - 1))
    owner = (iota((count, LANES), 0) & (per_block - 1)) // capacity
    lane = iota((count, LANES), 1)
    join = jnp.where(iota((2 * slots, LANES), 0) < slots, 32.0, 1.0).astype(BF16)

    @pl.loop(0, blocks // 2)
    def _(pair):
        for block in (2 * pair, 2 * pair + 1):
            tile = jnp.zeros((per_block, slots), jnp.int32)
            for b in range(devices_y):
                tile = jnp.where(row // capacity == b, cells[block * devices_y + b], tile)
            parts = [
                jnp.where(own_lane, part.astype(F32)[None], 0.0).reshape(count, slots).astype(BF16)
                for part in (tile >> 5, tile & 31)
            ]
            cell = dot(jnp.concatenate(parts, axis=1), join).astype(jnp.int32)
            place_x[block] = jnp.where(cell < 0, -1, cell & (cells_x - 1))
            at_j = onehot(lane == owner * cells_y + cell // cells_x)[:, :rows_j]
            for t in range(tracers):
                smooth_y[block, t] = lax.dot_general(
                    own_y[t], at_j, (((1,), (1,)), ((), ())), preferred_element_type=F32
                )

    def pick_rows(pair):
        for block in (2 * pair, 2 * pair + 1):
            column = place_x[block]
            at_i = jnp.concatenate(
                [onehot(column == lane + start) for start in range(0, cells_x, LANES)], axis=1
            )
            lines = pl.ds(pl.multiple_of(block * cells_x, cells_x), cells_x)
            target = pl.ds(pl.multiple_of(block * count, count), count)
            for t in range(tracers):
                picked_x[t, target, :] = dot(at_i, kernel_x_ref[t, lines, :]).astype(BF16)

    pl.loop(0, 1)(pick_rows)
    by_x.wait_recv()
    by_y.wait_recv()
    from_x, from_y = profiles.at[:, 1 - i1, i2, i3], profiles.at[:, i1, 1 - i2, i3]
    diagonals = [
        send(from_x.at[:, 0 : half // 2], along),
        send(from_y.at[:, half // 2 : half], across),
    ]
    to_twin += [send(from_x, twin), send(from_y, twin)]
    pl.loop(1, 2)(pick_rows)
    for copy in diagonals:
        copy.wait_recv()
    to_twin.append(send(profiles.at[:, 1 - i1, 1 - i2, i3], twin))
    pl.loop(2, blocks // 2)(pick_rows)
    for copy in to_twin:
        copy.wait_recv()

    pieces = half // per_block
    acc[...] = jnp.zeros_like(acc)
    level = iota((layers, LANES), 0)
    lane_of = iota((layers, LANES), 1)

    @pl.loop(0, blocks // 2)
    def _(pair):
        for n in range(2):
            block = 2 * pair + n
            piece = pl.multiple_of(lax.rem(block, pieces) * per_block, per_block)
            part = profiles[:, :, :, :, pl.ds(piece, per_block), :].reshape(count, LANES)
            base = lax.div(block, pieces) * layers
            turned[n] = lax.dot_general(
                onehot(lane_of == level + base),
                part,
                (((1,), (1,)), ((), ())),
                preferred_element_type=F32,
            )
        lines = pl.ds(pl.multiple_of(pair * (2 * count), 2 * count), 2 * count)
        for t in range(tracers):
            for n in range(2):
                weights = smooth_y[2 * pair + n, t]
                for k in range(levels):
                    r = t * levels + k
                    left[t, k * cells_y : (k + 1) * cells_y, n * count : (n + 1) * count] = (
                        weights * turned[n, r : r + 1, :]
                    ).astype(BF16)
            acc[t] += dot(left[t], picked_x[t, lines, :])

    mask = mask_ref[...].astype(F32)
    carried = [None] * tracers
    for k in range(levels):
        lines = slice(k * cells_y, (k + 1) * cells_y)
        for t in range(tracers):
            value = acc[t, lines, :]
            if k > 0:
                value += coef_ref[k] * carried[t]
            carried[t] = value * inverse[k]
            acc[t, lines, :] = carried[t]
    for k in range(levels - 1, -1, -1):
        lines = slice(k * cells_y, (k + 1) * cells_y)
        for t in range(tracers):
            if k + 1 < levels:
                carried[t] = acc[t, lines, :] + ratio[k] * carried[t]
            inc_ref[t * levels + k] = (carried[t] * mask).astype(BF16)

    store = pltpu.make_async_copy(inc_ref, inc_hbm, store_sem.at[0])
    store.start()
    field = inc_ref[...].reshape(layers * cells_y, cells_x)
    found = dot(field, at_own).reshape(layers, cells_y, slots)
    in_row = iota((1, cells_y, slots), 1) == cell_j[None]
    picked = jnp.sum(jnp.where(in_row, found, 0.0), axis=1)
    picked = jnp.concatenate([picked, jnp.zeros((slots - layers, slots), F32)], axis=0).T
    for d in range(devices):
        outgoing[d] = picked[d * capacity : (d + 1) * capacity]
    arrived[me] = outgoing[me]

    def back_copy(k):
        other, where = place(k)
        return pltpu.make_async_remote_copy(
            src_ref=outgoing.at[other],
            dst_ref=arrived.at[me],
            send_sem=back_send.at[k - 1],
            recv_sem=back_recv.at[k - 1],
            device_id=where,
            device_id_type=MESH,
        )

    @pl.loop(1, devices)
    def _(k):
        back_copy(k).start()

    for copy in sent:
        copy.wait_send()

    @pl.loop(1, devices)
    def _(k):
        cell_copy(k).wait_send()

    @pl.loop(1, devices)
    def _(k):
        back_copy(k).wait_recv()

    for d in range(devices):
        rows[d * capacity : (d + 1) * capacity] = arrived[d]
    equiv_ref[...] = jnp.where(live, rows[...].T[:layers], 0.0).astype(BF16)
    result = pltpu.make_async_copy(equiv_ref, equiv_hbm, store_sem.at[1])
    result.start()

    @pl.loop(1, devices)
    def _(k):
        back_copy(k).wait_send()

    store.wait()
    result.wait()


def body_gather(
    dims,
    innovations,
    station_columns,
    profile_counts,
    land_mask,
    vertical_coef,
    inverse_x,
    inverse_y,
):
    layers, slots = innovations.shape[1:]
    devices = profile_counts.shape[1]
    devices_y = dims[2] * dims[3]
    capacity = slots // devices
    cells_y, cells_x = land_mask.shape
    tracers = inverse_x.shape[0]
    levels = layers // tracers
    blocks = dims[0] * dims[1]
    count = devices * devices_y * capacity
    anywhere = pl.BlockSpec(memory_space=pl.ANY)
    operands = (
        innovations[0],
        station_columns,
        profile_counts,
        land_mask,
        vertical_coef,
        inverse_x,
        inverse_y,
    )
    n_profile = dims[0] - 1 + 8
    increment, equivalents = pl.pallas_call(
        functools.partial(profile_kernel, dims, capacity),
        out_shape=(
            jax.ShapeDtypeStruct((layers, cells_y, cells_x), BF16),
            jax.ShapeDtypeStruct((layers, slots), BF16),
        ),
        in_specs=[anywhere] * len(operands),
        out_specs=(anywhere, anywhere),
        scratch_shapes=[pltpu.VMEM(x.shape, x.dtype) for x in operands]
        + [
            pltpu.VMEM((devices, 1, slots), jnp.int32),
            pltpu.VMEM(dims + (slots // 2, LANES), BF16),
            pltpu.VMEM((blocks, count, LANES), jnp.int32),
            pltpu.VMEM((tracers, blocks * count, cells_x), BF16),
            pltpu.VMEM((blocks, tracers, cells_y, count), F32),
            pltpu.VMEM((tracers, levels * cells_y, 2 * count), BF16),
            pltpu.VMEM((2, layers, count), F32),
            pltpu.VMEM((tracers, levels * cells_y, cells_x), F32),
            pltpu.VMEM((levels, cells_y, cells_x), F32),
            pltpu.VMEM((levels, cells_y, cells_x), F32),
            pltpu.VMEM((layers, cells_y, cells_x), BF16),
            pltpu.VMEM((devices, capacity, LANES), F32),
            pltpu.VMEM((devices, capacity, LANES), F32),
            pltpu.VMEM((slots, LANES), F32),
            pltpu.VMEM((layers, slots), BF16),
            pltpu.SemaphoreType.DMA((len(operands),)),
            pltpu.SemaphoreType.DMA((2,)),
            pltpu.SemaphoreType.DMA((devices - 1,)),
            pltpu.SemaphoreType.DMA((devices - 1,)),
            pltpu.SemaphoreType.DMA((n_profile,)),
            pltpu.SemaphoreType.DMA((n_profile,)),
            pltpu.SemaphoreType.DMA((devices - 1,)),
            pltpu.SemaphoreType.DMA((devices - 1,)),
        ],
        compiler_params=pltpu.CompilerParams(
            collective_id=0, has_side_effects=True, vmem_limit_bytes=VMEM_BYTES
        ),
        name="smooth_profiles",
    )(*operands)
    parts = 4
    increment, equivalents = pl.pallas_call(
        functools.partial(hand_over_kernel, parts),
        out_shape=(
            jax.ShapeDtypeStruct(increment.shape, BF16),
            jax.ShapeDtypeStruct(equivalents.shape, BF16),
        ),
        in_specs=[anywhere] * 2,
        out_specs=(anywhere, anywhere),
        scratch_shapes=[pltpu.SemaphoreType.DMA((parts + 1,))],
        compiler_params=pltpu.CompilerParams(vmem_limit_bytes=VMEM_BYTES),
        name="hand_over",
    )(increment, equivalents)
    return increment, equivalents[None]


def hand_over_kernel(parts, inc_ref, equiv_ref, inc_out, equiv_out, sem):
    height = inc_ref.shape[0] // parts
    copies = [pltpu.make_async_copy(equiv_ref, equiv_out, sem.at[parts])]
    for k in range(parts):
        lines = pl.ds(k * height, height)
        copies.append(pltpu.make_async_copy(inc_ref.at[lines], inc_out.at[lines], sem.at[k]))
    for copy in copies:
        copy.start()
    for copy in copies:
        copy.wait()


def plan(devices_x, devices_y, innovations, land_mask, inverse_x, inverse_y):
    devices = devices_x * devices_y
    layers, slots = innovations.shape[1:]
    capacity = slots // devices
    cells_x = land_mask.shape[1] // devices_x
    fits = (
        slots == LANES
        and 2 * layers == LANES
        and capacity * devices_y == TILE
        and devices_x % 2 == 0
        and devices_y == 4
        and devices_x % 4 == 0
        and cells_x % LANES == 0
        and cells_x & (cells_x - 1) == 0
        and cells_x <= 32 * 256
        and inverse_y.shape[1] <= LANES
    )
    return (devices_x // 2, 2, devices_y // 2, 2) if fits else None


def solution(mesh):
    in_specs = (
        P(("gx", "gy"), None, None),
        P(("gx", "gy"), None),
        P(("gx", "gy"), None),
        P("gy", "gx"),
        P(None, "gy", "gx"),
        P(None, None, "gx"),
        P(),
    )
    out_specs = (P(None, "gy", "gx"), P(("gx", "gy"), None, None))

    def run(innovations, columns, counts, land_mask, coef, inverse_x, inverse_y):
        dims = plan(
            mesh.shape["gx"], mesh.shape["gy"], innovations, land_mask, inverse_x, inverse_y
        )
        body = body_exchange if dims is None else functools.partial(body_gather, dims)
        return jax.shard_map(
            body, mesh=mesh, in_specs=in_specs, out_specs=out_specs, check_vma=False
        )(innovations, columns, counts, land_mask, coef, inverse_x, inverse_y)

    return run
```

```python
import functools
import jax
import jax.numpy as jnp
from jax import lax
from jax.experimental import pallas as pl
from jax.experimental.pallas import tpu as pltpu
from jax.sharding import PartitionSpec as P

LEV = 32
LANES = 128
TILE = 16
VMEM_BYTES = 56 << 20
MESH = pl.DeviceIdType.MESH
F32 = jnp.float32
BF16 = jnp.bfloat16


def vertical_solve(rhs_field, coupling):
    levels = coupling.shape[0]
    zero_row = jnp.zeros_like(coupling[0])
    ratios = []
    partial_sol = []
    for level in range(levels):
        upper_coef = coupling[level + 1] if level + 1 < levels else zero_row
        diagonal = 1.0 + coupling[level] + upper_coef
        if level == 0:
            denominator = diagonal
            carried = rhs_field[:, 0]
        else:
            denominator = diagonal + coupling[level] * ratios[-1]
            carried = rhs_field[:, level] + coupling[level] * partial_sol[-1]
        ratios.append(-upper_coef / denominator)
        partial_sol.append(carried / denominator)
    solution = [partial_sol[-1]]
    for level in range(levels - 2, -1, -1):
        solution.append(partial_sol[level] - ratios[level] * solution[-1])
    return jnp.stack(solution[::-1], axis=1)


def body_exchange(
    innovations, station_columns, profile_counts, land_mask, vertical_coef, inverse_x, inverse_y
):
    layers = innovations.shape[1]
    devices_all = lax.axis_size(("gx", "gy"))
    devices_y = lax.axis_size("gy")
    capacity = innovations.shape[2] // devices_all
    slots = devices_all * capacity
    cells_y, cells_x = land_mask.shape
    cell_count = cells_y * cells_x
    tracers = inverse_x.shape[0]
    slot_index = lax.broadcasted_iota(jnp.int32, (devices_all, capacity), 1)
    live_flat = (slot_index < profile_counts[0][:, None]).reshape(slots)
    outgoing = jnp.where(live_flat[None, None, :], innovations, jnp.zeros((), jnp.bfloat16))
    arrived = lax.all_to_all(
        outgoing.reshape(layers, 1, devices_all, capacity),
        ("gx", "gy"),
        split_axis=2,
        concat_axis=1,
        tiled=True,
    )
    arrived = arrived.reshape(layers, slots)
    columns = station_columns[0]
    mask_flat = land_mask.reshape(cell_count)
    sea_slot = mask_flat[columns] > 0
    line_values = jnp.where(sea_slot[None, :], arrived, jnp.zeros((), jnp.bfloat16))
    line_columns = columns.reshape(1, slots)
    empty = jnp.zeros((tracers, layers // tracers, cells_y, cells_x), jnp.float32)
    values_piece = lax.all_gather(line_values, "gx", axis=1, tiled=True)
    columns_piece = lax.all_gather(line_columns, "gx", axis=1, tiled=True)
    sources = values_piece.shape[1] // slots

    def one_source(k, accum):
        block_values = lax.dynamic_slice_in_dim(values_piece, k * slots, slots, 1)
        block_columns = lax.dynamic_slice_in_dim(columns_piece, k * slots, slots, 1)[0]
        dense = (
            jnp.zeros((layers, cell_count), jnp.float32)
            .at[:, block_columns]
            .add(block_values.astype(jnp.float32))
        )
        dense = dense.astype(jnp.bfloat16).reshape(tracers, layers // tracers, cells_y, cells_x)
        source = k * slots // slots
        kernel_rows = lax.dynamic_slice_in_dim(inverse_x, source * cells_x, cells_x, 1)
        return accum + jnp.einsum(
            "tkjn,tnm->tkjm", dense, kernel_rows, preferred_element_type=jnp.float32
        )

    summed_x = lax.fori_loop(0, sources, one_source, empty)
    along_x = summed_x.astype(jnp.bfloat16).reshape(layers, cells_y, cells_x)
    rows_y = layers // devices_y
    tracer_y = lax.axis_index("gy") * rows_y // LEV
    matrix_y = lax.dynamic_index_in_dim(inverse_y, tracer_y, 0, keepdims=False)
    product = jnp.einsum(
        "rjc,jm->rmc",
        lax.all_to_all(along_x, "gy", split_axis=0, concat_axis=1, tiled=True),
        matrix_y,
        preferred_element_type=jnp.float32,
    ).astype(jnp.bfloat16)
    along_y = lax.all_to_all(product, "gy", split_axis=1, concat_axis=0, tiled=True)
    mask_field = mask_flat.astype(jnp.float32)
    column_field = along_y.astype(jnp.float32).reshape(2, LEV, cell_count)
    solved = vertical_solve(column_field, vertical_coef.reshape(LEV, cell_count))
    increment = (
        (solved * mask_field[None, None, :]).astype(jnp.bfloat16).reshape(layers, cells_y, cells_x)
    )
    picked = increment.reshape(layers, cell_count)[:, columns]
    returned = lax.all_to_all(
        picked.reshape(layers, 1, devices_all, capacity),
        ("gx", "gy"),
        split_axis=2,
        concat_axis=1,
        tiled=True,
    )
    returned = returned.reshape(1, layers, slots)
    equivalents = jnp.where(live_flat[None, None, :], returned, jnp.zeros((), jnp.bfloat16))
    return (increment, equivalents)


def iota(shape, dim):
    return lax.broadcasted_iota(jnp.int32, shape, dim)


def onehot(condition):
    return jnp.where(condition, 1.0, 0.0).astype(BF16)


def dot(a, b):
    return jnp.dot(a, b, preferred_element_type=F32)


def profile_kernel(
    dims,
    capacity,
    innov_hbm,
    columns_hbm,
    counts_hbm,
    mask_hbm,
    coef_hbm,
    kernel_x_hbm,
    kernel_y_hbm,
    inc_hbm,
    equiv_hbm,
    innov_ref,
    columns_ref,
    counts_ref,
    mask_ref,
    coef_ref,
    kernel_x_ref,
    kernel_y_ref,
    cells,
    profiles,
    place_x,
    picked_x,
    smooth_y,
    left,
    turned,
    acc,
    inverse,
    ratio,
    inc_ref,
    outgoing,
    arrived,
    rows,
    equiv_ref,
    load_sem,
    store_sem,
    cell_send,
    cell_recv,
    prof_send,
    prof_recv,
    back_send,
    back_recv,
):
    gx_outer, gx_inner, gy_outer, gy_inner = dims
    blocks, devices_y = gx_outer * gx_inner, gy_outer * gy_inner
    gx, gy = lax.axis_index("gx"), lax.axis_index("gy")
    i0, i1 = gx // gx_inner, lax.rem(gx, gx_inner)
    i2, i3 = gy // gy_inner, lax.rem(gy, gy_inner)
    me = gx * devices_y + gy
    layers, slots = innov_ref.shape
    devices = blocks * devices_y
    levels, cells_y, cells_x = coef_ref.shape
    tracers, rows_j, _ = kernel_y_ref.shape
    per_block = devices_y * capacity
    count = devices * per_block

    loads = [
        pltpu.make_async_copy(source, target, load_sem.at[k])
        for k, (source, target) in enumerate(
            [
                (columns_hbm, columns_ref),
                (mask_hbm, mask_ref),
                (counts_hbm, counts_ref),
                (innov_hbm, innov_ref),
                (coef_hbm, coef_ref),
                (kernel_y_hbm, kernel_y_ref),
                (kernel_x_hbm, kernel_x_ref),
            ]
        )
    ]
    for load in loads:
        load.start()

    def place(k):
        other = lax.rem(me + k, devices)
        return other, (lax.div(other, devices_y), lax.rem(other, devices_y))

    barrier = pltpu.get_barrier_semaphore()

    places = [place(k) for k in range(1, devices)]
    for _, where in places:
        pl.semaphore_signal(barrier, inc=1, device_id=where, device_id_type=MESH)

    loads[0].wait()
    loads[1].wait()
    columns = columns_ref[...]
    cell_i, cell_j = columns & (cells_x - 1), columns // cells_x
    at_own = onehot(iota((cells_x, slots), 0) == cell_i)
    masks = dot(mask_ref[...].astype(F32).astype(BF16), at_own)
    sea = jnp.sum(jnp.where(iota((cells_y, slots), 0) == cell_j, masks, 0.0), 0, keepdims=True)
    cells[me] = jnp.where(sea > 0.0, columns, -1)
    pl.semaphore_wait(barrier, devices - 1)

    for _, where in places:
        pltpu.make_async_remote_copy(
            src_ref=cells.at[me],
            dst_ref=cells.at[me],
            send_sem=cell_send,
            recv_sem=cell_recv,
            device_id=where,
            device_id_type=MESH,
        ).start()

    def all_of(ref, sem):
        others = ref.at[pl.ds(0, devices - 1)]
        return pltpu.make_async_copy(others, others, sem)

    loads[2].wait()
    loads[3].wait()
    counts = jnp.broadcast_to(counts_ref[...].astype(F32), (8, devices)).astype(BF16)
    lane_count = dot(
        counts, onehot(iota((devices, slots), 0) == iota((devices, slots), 1) // capacity)
    )[0:1]
    live = (iota((1, slots), 1) & (capacity - 1)).astype(F32) < lane_count
    values = jnp.where(live, innov_ref[...].astype(F32), 0.0)
    half = slots // 2
    packed = jnp.concatenate([values, pltpu.roll(values, half, 1)], axis=0).T
    profiles[i0, i1, i2, i3] = packed[0:half].astype(BF16)

    sent = []

    def send(block, partner):
        copy = pltpu.make_async_remote_copy(
            src_ref=block,
            dst_ref=block,
            send_sem=prof_send.at[len(sent)],
            recv_sem=prof_recv.at[len(sent)],
            device_id=partner,
            device_id_type=MESH,
        )
        copy.start()
        sent.append(copy)
        return copy

    across = (i0 * gx_inner + (1 - i1), gy)
    along = (gx, (1 - i2) * gy_inner + i3)
    twin = (gx, i2 * gy_inner + (1 - i3))
    far = [
        send(
            profiles.at[i0, i1, i2, i3],
            (lax.rem(i0 + k, gx_outer) * gx_inner + i1, gy),
        )
        for k in range(1, gx_outer)
    ]

    loads[4].wait()
    last = None
    for k in range(levels):
        diagonal = 1.0 + coef_ref[k]
        if k + 1 < levels:
            diagonal += coef_ref[k + 1]
        if k > 0:
            diagonal -= coef_ref[k] * last
        inv = 1.0 / diagonal
        inverse[k] = inv
        if k + 1 < levels:
            last = coef_ref[k + 1] * inv
            ratio[k] = last

    for copy in far:
        copy.wait_recv()
    own_line = profiles.at[:, i1, i2, i3]
    by_x = send(own_line, across)
    by_y = send(own_line, along)
    to_twin = [send(own_line, twin)]

    all_of(cells, cell_recv).wait()

    loads[5].wait()
    loads[6].wait()
    own_rows = onehot(iota((cells_y, rows_j), 1) == gy * cells_y + iota((cells_y, rows_j), 0))
    own_y = [
        lax.dot_general(
            own_rows, kernel_y_ref[t], (((1,), (1,)), ((), ())), preferred_element_type=F32
        ).astype(BF16)
        for t in range(tracers)
    ]
    row = iota((per_block, slots), 0)
    shape = (devices, per_block, slots)
    own_lane = iota(shape, 2) == iota(shape, 0) * capacity + (iota(shape, 1) & (capacity - 1))
    owner = (iota((count, LANES), 0) & (per_block - 1)) // capacity
    lane = iota((count, LANES), 1)
    join = jnp.where(iota((2 * slots, LANES), 0) < slots, 32.0, 1.0).astype(BF16)

    @pl.loop(0, blocks // 2)
    def _(pair):
        for block in (2 * pair, 2 * pair + 1):
            tile = jnp.zeros((per_block, slots), jnp.int32)
            for b in range(devices_y):
                tile = jnp.where(row // capacity == b, cells[block * devices_y + b], tile)
            parts = [
                jnp.where(own_lane, part.astype(F32)[None], 0.0).reshape(count, slots).astype(BF16)
                for part in (tile >> 5, tile & 31)
            ]
            cell = dot(jnp.concatenate(parts, axis=1), join).astype(jnp.int32)
            place_x[block] = jnp.where(cell < 0, -1, cell & (cells_x - 1))
            at_j = onehot(lane == owner * cells_y + cell // cells_x)[:, :rows_j]
            for t in range(tracers):
                smooth_y[block, t] = lax.dot_general(
                    own_y[t], at_j, (((1,), (1,)), ((), ())), preferred_element_type=F32
                )

    def pick_rows(pair):
        for block in (2 * pair, 2 * pair + 1):
            column = place_x[block]
            at_i = jnp.concatenate(
                [onehot(column == lane + start) for start in range(0, cells_x, LANES)], axis=1
            )
            lines = pl.ds(pl.multiple_of(block * cells_x, cells_x), cells_x)
            target = pl.ds(pl.multiple_of(block * count, count), count)
            for t in range(tracers):
                picked_x[t, target, :] = dot(at_i, kernel_x_ref[t, lines, :]).astype(BF16)

    pl.loop(0, 1)(pick_rows)
    by_x.wait_recv()
    by_y.wait_recv()
    from_x, from_y = profiles.at[:, 1 - i1, i2, i3], profiles.at[:, i1, 1 - i2, i3]
    diagonals = [
        send(from_x.at[:, 0 : half // 2], along),
        send(from_y.at[:, half // 2 : half], across),
    ]
    to_twin += [send(from_x, twin), send(from_y, twin)]
    pl.loop(1, 2)(pick_rows)
    for copy in diagonals:
        copy.wait_recv()
    to_twin.append(send(profiles.at[:, 1 - i1, 1 - i2, i3], twin))
    pl.loop(2, blocks // 2)(pick_rows)
    for copy in to_twin:
        copy.wait_recv()

    pieces = half // per_block
    acc[...] = jnp.zeros_like(acc)
    level = iota((layers, LANES), 0)
    lane_of = iota((layers, LANES), 1)

    @pl.loop(0, blocks // 2)
    def _(pair):
        for n in range(2):
            block = 2 * pair + n
            piece = pl.multiple_of(lax.rem(block, pieces) * per_block, per_block)
            part = profiles[:, :, :, :, pl.ds(piece, per_block), :].reshape(count, LANES)
            base = lax.div(block, pieces) * layers
            turned[n] = lax.dot_general(
                onehot(lane_of == level + base),
                part,
                (((1,), (1,)), ((), ())),
                preferred_element_type=F32,
            )
        lines = pl.ds(pl.multiple_of(pair * (2 * count), 2 * count), 2 * count)
        for t in range(tracers):
            for n in range(2):
                weights = smooth_y[2 * pair + n, t]
                for k in range(levels):
                    r = t * levels + k
                    left[t, k * cells_y : (k + 1) * cells_y, n * count : (n + 1) * count] = (
                        weights * turned[n, r : r + 1, :]
                    ).astype(BF16)
            acc[t] += dot(left[t], picked_x[t, lines, :])

    mask = mask_ref[...].astype(F32)
    carried = [None] * tracers
    for k in range(levels):
        lines = slice(k * cells_y, (k + 1) * cells_y)
        for t in range(tracers):
            value = acc[t, lines, :]
            if k > 0:
                value += coef_ref[k] * carried[t]
            carried[t] = value * inverse[k]
            acc[t, lines, :] = carried[t]
    for k in range(levels - 1, -1, -1):
        lines = slice(k * cells_y, (k + 1) * cells_y)
        for t in range(tracers):
            if k + 1 < levels:
                carried[t] = acc[t, lines, :] + ratio[k] * carried[t]
            inc_ref[t * levels + k] = (carried[t] * mask).astype(BF16)

    store = pltpu.make_async_copy(inc_ref, inc_hbm, store_sem.at[0])
    store.start()
    field = inc_ref[...].reshape(layers * cells_y, cells_x)
    found = dot(field, at_own).reshape(layers, cells_y, slots)
    in_row = iota((1, cells_y, slots), 1) == cell_j[None]
    picked = jnp.sum(jnp.where(in_row, found, 0.0), axis=1)
    picked = jnp.concatenate([picked, jnp.zeros((slots - layers, slots), F32)], axis=0).T
    for d in range(devices):
        outgoing[d] = picked[d * capacity : (d + 1) * capacity]
    arrived[me] = outgoing[me]

    for other, where in places:
        pltpu.make_async_remote_copy(
            src_ref=outgoing.at[other],
            dst_ref=arrived.at[me],
            send_sem=back_send,
            recv_sem=back_recv,
            device_id=where,
            device_id_type=MESH,
        ).start()
    for copy in sent:
        copy.wait_send()
    all_of(cells, cell_send).wait()
    all_of(arrived, back_recv).wait()
    for d in range(devices):
        rows[d * capacity : (d + 1) * capacity] = arrived[d]
    equiv_ref[...] = jnp.where(live, rows[...].T[:layers], 0.0).astype(BF16)
    result = pltpu.make_async_copy(equiv_ref, equiv_hbm, store_sem.at[1])
    result.start()

    all_of(outgoing, back_send).wait()
    store.wait()
    result.wait()


def body_gather(
    dims,
    innovations,
    station_columns,
    profile_counts,
    land_mask,
    vertical_coef,
    inverse_x,
    inverse_y,
):
    layers, slots = innovations.shape[1:]
    devices = profile_counts.shape[1]
    devices_y = dims[2] * dims[3]
    capacity = slots // devices
    cells_y, cells_x = land_mask.shape
    tracers = inverse_x.shape[0]
    levels = layers // tracers
    blocks = dims[0] * dims[1]
    count = devices * devices_y * capacity
    anywhere = pl.BlockSpec(memory_space=pl.ANY)
    operands = (
        innovations[0],
        station_columns,
        profile_counts,
        land_mask,
        vertical_coef,
        inverse_x,
        inverse_y,
    )
    n_profile = dims[0] - 1 + 8
    increment, equivalents = pl.pallas_call(
        functools.partial(profile_kernel, dims, capacity),
        out_shape=(
            jax.ShapeDtypeStruct((layers, cells_y, cells_x), BF16),
            jax.ShapeDtypeStruct((layers, slots), BF16),
        ),
        in_specs=[anywhere] * len(operands),
        out_specs=(anywhere, anywhere),
        scratch_shapes=[pltpu.VMEM(x.shape, x.dtype) for x in operands]
        + [
            pltpu.VMEM((devices, 1, slots), jnp.int32),
            pltpu.VMEM(dims + (slots // 2, LANES), BF16),
            pltpu.VMEM((blocks, count, LANES), jnp.int32),
            pltpu.VMEM((tracers, blocks * count, cells_x), BF16),
            pltpu.VMEM((blocks, tracers, cells_y, count), F32),
            pltpu.VMEM((tracers, levels * cells_y, 2 * count), BF16),
            pltpu.VMEM((2, layers, count), F32),
            pltpu.VMEM((tracers, levels * cells_y, cells_x), F32),
            pltpu.VMEM((levels, cells_y, cells_x), F32),
            pltpu.VMEM((levels, cells_y, cells_x), F32),
            pltpu.VMEM((layers, cells_y, cells_x), BF16),
            pltpu.VMEM((devices, capacity, LANES), F32),
            pltpu.VMEM((devices, capacity, LANES), F32),
            pltpu.VMEM((slots, LANES), F32),
            pltpu.VMEM((layers, slots), BF16),
            pltpu.SemaphoreType.DMA((len(operands),)),
            pltpu.SemaphoreType.DMA((2,)),
            pltpu.SemaphoreType.DMA,
            pltpu.SemaphoreType.DMA,
            pltpu.SemaphoreType.DMA((n_profile,)),
            pltpu.SemaphoreType.DMA((n_profile,)),
            pltpu.SemaphoreType.DMA,
            pltpu.SemaphoreType.DMA,
        ],
        compiler_params=pltpu.CompilerParams(
            collective_id=0, has_side_effects=True, vmem_limit_bytes=VMEM_BYTES
        ),
        name="smooth_profiles",
    )(*operands)
    parts = 4
    increment, equivalents = pl.pallas_call(
        functools.partial(hand_over_kernel, parts),
        out_shape=(
            jax.ShapeDtypeStruct(increment.shape, BF16),
            jax.ShapeDtypeStruct(equivalents.shape, BF16),
        ),
        in_specs=[anywhere] * 2,
        out_specs=(anywhere, anywhere),
        scratch_shapes=[
            pltpu.VMEM(increment.shape, BF16),
            pltpu.VMEM(equivalents.shape, BF16),
            pltpu.SemaphoreType.DMA((2 * (parts + 1),)),
        ],
        compiler_params=pltpu.CompilerParams(vmem_limit_bytes=VMEM_BYTES),
        name="hand_over",
    )(increment, equivalents)
    return increment, equivalents[None]


def hand_over_kernel(parts, inc_ref, equiv_ref, inc_out, equiv_out, inc_held, equiv_held, sem):
    height = inc_ref.shape[0] // parts
    steps = [(equiv_ref, equiv_held, equiv_out)]
    for k in range(parts):
        lines = pl.ds(k * height, height)
        steps.append((inc_ref.at[lines], inc_held.at[lines], inc_out.at[lines]))
    n = len(steps)
    ins = [pltpu.make_async_copy(a, b, sem.at[k]) for k, (a, b, _) in enumerate(steps)]
    outs = [pltpu.make_async_copy(b, c, sem.at[n + k]) for k, (_, b, c) in enumerate(steps)]
    for copy in ins:
        copy.start()
    for first, second in zip(ins, outs):
        first.wait()
        second.start()
    for copy in outs:
        copy.wait()


def plan(devices_x, devices_y, innovations, land_mask, inverse_x, inverse_y):
    devices = devices_x * devices_y
    layers, slots = innovations.shape[1:]
    capacity = slots // devices
    cells_x = land_mask.shape[1] // devices_x
    fits = (
        slots == LANES
        and 2 * layers == LANES
        and capacity * devices_y == TILE
        and devices_x % 2 == 0
        and devices_y == 4
        and devices_x % 4 == 0
        and cells_x % LANES == 0
        and cells_x & (cells_x - 1) == 0
        and cells_x <= 32 * 256
        and inverse_y.shape[1] <= LANES
    )
    return (devices_x // 2, 2, devices_y // 2, 2) if fits else None


def solution(mesh):
    in_specs = (
        P(("gx", "gy"), None, None),
        P(("gx", "gy"), None),
        P(("gx", "gy"), None),
        P("gy", "gx"),
        P(None, "gy", "gx"),
        P(None, None, "gx"),
        P(),
    )
    out_specs = (P(None, "gy", "gx"), P(("gx", "gy"), None, None))

    def run(innovations, columns, counts, land_mask, coef, inverse_x, inverse_y):
        dims = plan(
            mesh.shape["gx"], mesh.shape["gy"], innovations, land_mask, inverse_x, inverse_y
        )
        body = body_exchange if dims is None else functools.partial(body_gather, dims)
        return jax.shard_map(
            body, mesh=mesh, in_specs=in_specs, out_specs=out_specs, check_vma=False
        )(innovations, columns, counts, land_mask, coef, inverse_x, inverse_y)

    return run
```

```python
import functools
import jax
import jax.numpy as jnp
from jax import lax
from jax.experimental import pallas as pl
from jax.experimental.pallas import tpu as pltpu
from jax.sharding import PartitionSpec as P

LEV = 32
LANES = 128
TILE = 16
VMEM_BYTES = 56 << 20
MESH = pl.DeviceIdType.MESH
F32 = jnp.float32
BF16 = jnp.bfloat16


def vertical_solve(rhs_field, coupling):
    levels = coupling.shape[0]
    zero_row = jnp.zeros_like(coupling[0])
    ratios = []
    partial_sol = []
    for level in range(levels):
        upper_coef = coupling[level + 1] if level + 1 < levels else zero_row
        diagonal = 1.0 + coupling[level] + upper_coef
        if level == 0:
            denominator = diagonal
            carried = rhs_field[:, 0]
        else:
            denominator = diagonal + coupling[level] * ratios[-1]
            carried = rhs_field[:, level] + coupling[level] * partial_sol[-1]
        ratios.append(-upper_coef / denominator)
        partial_sol.append(carried / denominator)
    solution = [partial_sol[-1]]
    for level in range(levels - 2, -1, -1):
        solution.append(partial_sol[level] - ratios[level] * solution[-1])
    return jnp.stack(solution[::-1], axis=1)


def body_exchange(
    innovations, station_columns, profile_counts, land_mask, vertical_coef, inverse_x, inverse_y
):
    layers = innovations.shape[1]
    devices_all = lax.axis_size(("gx", "gy"))
    devices_y = lax.axis_size("gy")
    capacity = innovations.shape[2] // devices_all
    slots = devices_all * capacity
    cells_y, cells_x = land_mask.shape
    cell_count = cells_y * cells_x
    tracers = inverse_x.shape[0]
    slot_index = lax.broadcasted_iota(jnp.int32, (devices_all, capacity), 1)
    live_flat = (slot_index < profile_counts[0][:, None]).reshape(slots)
    outgoing = jnp.where(live_flat[None, None, :], innovations, jnp.zeros((), jnp.bfloat16))
    arrived = lax.all_to_all(
        outgoing.reshape(layers, 1, devices_all, capacity),
        ("gx", "gy"),
        split_axis=2,
        concat_axis=1,
        tiled=True,
    )
    arrived = arrived.reshape(layers, slots)
    columns = station_columns[0]
    mask_flat = land_mask.reshape(cell_count)
    sea_slot = mask_flat[columns] > 0
    line_values = jnp.where(sea_slot[None, :], arrived, jnp.zeros((), jnp.bfloat16))
    line_columns = columns.reshape(1, slots)
    empty = jnp.zeros((tracers, layers // tracers, cells_y, cells_x), jnp.float32)
    values_piece = lax.all_gather(line_values, "gx", axis=1, tiled=True)
    columns_piece = lax.all_gather(line_columns, "gx", axis=1, tiled=True)
    sources = values_piece.shape[1] // slots

    def one_source(k, accum):
        block_values = lax.dynamic_slice_in_dim(values_piece, k * slots, slots, 1)
        block_columns = lax.dynamic_slice_in_dim(columns_piece, k * slots, slots, 1)[0]
        dense = (
            jnp.zeros((layers, cell_count), jnp.float32)
            .at[:, block_columns]
            .add(block_values.astype(jnp.float32))
        )
        dense = dense.astype(jnp.bfloat16).reshape(tracers, layers // tracers, cells_y, cells_x)
        source = k * slots // slots
        kernel_rows = lax.dynamic_slice_in_dim(inverse_x, source * cells_x, cells_x, 1)
        return accum + jnp.einsum(
            "tkjn,tnm->tkjm", dense, kernel_rows, preferred_element_type=jnp.float32
        )

    summed_x = lax.fori_loop(0, sources, one_source, empty)
    along_x = summed_x.astype(jnp.bfloat16).reshape(layers, cells_y, cells_x)
    rows_y = layers // devices_y
    tracer_y = lax.axis_index("gy") * rows_y // LEV
    matrix_y = lax.dynamic_index_in_dim(inverse_y, tracer_y, 0, keepdims=False)
    product = jnp.einsum(
        "rjc,jm->rmc",
        lax.all_to_all(along_x, "gy", split_axis=0, concat_axis=1, tiled=True),
        matrix_y,
        preferred_element_type=jnp.float32,
    ).astype(jnp.bfloat16)
    along_y = lax.all_to_all(product, "gy", split_axis=1, concat_axis=0, tiled=True)
    mask_field = mask_flat.astype(jnp.float32)
    column_field = along_y.astype(jnp.float32).reshape(2, LEV, cell_count)
    solved = vertical_solve(column_field, vertical_coef.reshape(LEV, cell_count))
    increment = (
        (solved * mask_field[None, None, :]).astype(jnp.bfloat16).reshape(layers, cells_y, cells_x)
    )
    picked = increment.reshape(layers, cell_count)[:, columns]
    returned = lax.all_to_all(
        picked.reshape(layers, 1, devices_all, capacity),
        ("gx", "gy"),
        split_axis=2,
        concat_axis=1,
        tiled=True,
    )
    returned = returned.reshape(1, layers, slots)
    equivalents = jnp.where(live_flat[None, None, :], returned, jnp.zeros((), jnp.bfloat16))
    return (increment, equivalents)


def iota(shape, dim):
    return lax.broadcasted_iota(jnp.int32, shape, dim)


def onehot(condition):
    return jnp.where(condition, 1.0, 0.0).astype(BF16)


def dot(a, b):
    return jnp.dot(a, b, preferred_element_type=F32)


def profile_kernel(
    dims,
    capacity,
    innov_hbm,
    columns_hbm,
    counts_hbm,
    mask_hbm,
    coef_hbm,
    kernel_x_hbm,
    kernel_y_hbm,
    inc_hbm,
    equiv_hbm,
    innov_ref,
    columns_ref,
    counts_ref,
    mask_ref,
    coef_ref,
    kernel_x_ref,
    kernel_y_ref,
    cells,
    profiles,
    place_x,
    picked_x,
    smooth_y,
    left,
    turned,
    acc,
    inverse,
    ratio,
    inc_ref,
    outgoing,
    arrived,
    rows,
    equiv_ref,
    load_sem,
    store_sem,
    cell_send,
    cell_recv,
    prof_send,
    prof_recv,
    back_send,
    back_recv,
):
    gx_outer, gx_inner, gy_outer, gy_inner = dims
    blocks, devices_y = gx_outer * gx_inner, gy_outer * gy_inner
    gx, gy = lax.axis_index("gx"), lax.axis_index("gy")
    i0, i1 = gx // gx_inner, lax.rem(gx, gx_inner)
    i2, i3 = gy // gy_inner, lax.rem(gy, gy_inner)
    me = gx * devices_y + gy
    layers, slots = innov_ref.shape
    devices = blocks * devices_y
    levels, cells_y, cells_x = coef_ref.shape
    tracers, rows_j, _ = kernel_y_ref.shape
    per_block = devices_y * capacity
    count = devices * per_block
    by_capacity, by_cells_x = capacity.bit_length() - 1, cells_x.bit_length() - 1

    loads = [
        pltpu.make_async_copy(source, target, load_sem.at[k])
        for k, (source, target) in enumerate(
            [
                (columns_hbm, columns_ref),
                (mask_hbm, mask_ref),
                (counts_hbm, counts_ref),
                (innov_hbm, innov_ref),
                (coef_hbm, coef_ref),
                (kernel_y_hbm, kernel_y_ref),
                (kernel_x_hbm, kernel_x_ref),
            ]
        )
    ]
    for load in loads:
        load.start()

    def place(k):
        other = lax.rem(me + k, devices)
        return other, (lax.div(other, devices_y), lax.rem(other, devices_y))

    barrier = pltpu.get_barrier_semaphore()

    places = [place(k) for k in range(1, devices)]
    for _, where in places:
        pl.semaphore_signal(barrier, inc=1, device_id=where, device_id_type=MESH)

    loads[0].wait()
    loads[1].wait()
    columns = columns_ref[...]
    cell_i, cell_j = columns & (cells_x - 1), columns >> by_cells_x
    at_own = onehot(iota((cells_x, slots), 0) == cell_i)
    masks = dot(mask_ref[...].astype(F32).astype(BF16), at_own)
    sea = jnp.sum(jnp.where(iota((cells_y, slots), 0) == cell_j, masks, 0.0), 0, keepdims=True)
    cells[me] = jnp.where(sea > 0.0, columns, -1)
    pl.semaphore_wait(barrier, devices - 1)

    for _, where in places:
        pltpu.make_async_remote_copy(
            src_ref=cells.at[me],
            dst_ref=cells.at[me],
            send_sem=cell_send,
            recv_sem=cell_recv,
            device_id=where,
            device_id_type=MESH,
        ).start()

    def all_of(ref, sem):
        others = ref.at[pl.ds(0, devices - 1)]
        return pltpu.make_async_copy(others, others, sem)

    loads[2].wait()
    loads[3].wait()
    counts = jnp.broadcast_to(counts_ref[...].astype(F32), (8, devices)).astype(BF16)
    lane_count = dot(
        counts, onehot(iota((devices, slots), 0) == iota((devices, slots), 1) >> by_capacity)
    )[0:1]
    live = (iota((1, slots), 1) & (capacity - 1)).astype(F32) < lane_count
    values = jnp.where(live, innov_ref[...].astype(F32), 0.0)
    half = slots // 2
    packed = jnp.concatenate([values, pltpu.roll(values, half, 1)], axis=0).T
    profiles[i0, i1, i2, i3] = packed[0:half].astype(BF16)

    sent = []

    def send(block, partner):
        copy = pltpu.make_async_remote_copy(
            src_ref=block,
            dst_ref=block,
            send_sem=prof_send.at[len(sent)],
            recv_sem=prof_recv.at[len(sent)],
            device_id=partner,
            device_id_type=MESH,
        )
        copy.start()
        sent.append(copy)
        return copy

    across = (i0 * gx_inner + (1 - i1), gy)
    along = (gx, (1 - i2) * gy_inner + i3)
    twin = (gx, i2 * gy_inner + (1 - i3))
    far = [
        send(
            profiles.at[i0, i1, i2, i3],
            (lax.rem(i0 + k, gx_outer) * gx_inner + i1, gy),
        )
        for k in range(1, gx_outer)
    ]

    loads[4].wait()
    last = None
    for k in range(levels):
        diagonal = 1.0 + coef_ref[k]
        if k + 1 < levels:
            diagonal += coef_ref[k + 1]
        if k > 0:
            diagonal -= coef_ref[k] * last
        inv = 1.0 / diagonal
        inverse[k] = inv
        if k + 1 < levels:
            last = coef_ref[k + 1] * inv
            ratio[k] = last

    for copy in far:
        copy.wait_recv()
    own_line = profiles.at[:, i1, i2, i3]
    by_x = send(own_line, across)
    by_y = send(own_line, along)
    to_twin = [send(own_line, twin)]

    all_of(cells, cell_recv).wait()

    loads[5].wait()
    loads[6].wait()
    own_rows = onehot(iota((cells_y, rows_j), 1) == gy * cells_y + iota((cells_y, rows_j), 0))
    own_y = [
        lax.dot_general(
            own_rows, kernel_y_ref[t], (((1,), (1,)), ((), ())), preferred_element_type=F32
        ).astype(BF16)
        for t in range(tracers)
    ]
    row, lane = iota((per_block, LANES), 0), iota((per_block, LANES), 1)
    owner = row >> by_capacity
    first_lane = lane - (row & (capacity - 1))
    row_lane = lane - owner * cells_y
    sender = iota((devices, 1, 1), 0) * capacity
    join = jnp.where(iota((2 * slots, LANES), 0) < slots, 32.0, 1.0).astype(BF16)

    @pl.loop(0, blocks // 2)
    def _(pair):
        for block in (2 * pair, 2 * pair + 1):
            tile = jnp.zeros((per_block, slots), jnp.int32)
            for b in range(devices_y):
                tile = jnp.where(owner == b, cells[block * devices_y + b], tile)
            own_lane = first_lane[None] == sender
            parts = [
                jnp.where(own_lane, part.astype(F32)[None], 0.0).reshape(count, slots).astype(BF16)
                for part in (tile >> 5, tile & 31)
            ]
            cell = dot(jnp.concatenate(parts, axis=1), join).astype(jnp.int32)
            place_x[block] = jnp.where(cell < 0, -1, cell & (cells_x - 1))
            cell_rows = (cell >> by_cells_x).reshape(devices, per_block, LANES)
            at_j = onehot(cell_rows == row_lane[None]).reshape(count, LANES)[:, :rows_j]
            for t in range(tracers):
                smooth_y[block, t] = lax.dot_general(
                    own_y[t], at_j, (((1,), (1,)), ((), ())), preferred_element_type=F32
                ).astype(BF16)

    def pick_rows(pair):
        lane_row = iota((1, LANES), 1)
        for block in (2 * pair, 2 * pair + 1):
            column = place_x[block]
            at_i = jnp.concatenate(
                [onehot(column == lane_row + start) for start in range(0, cells_x, LANES)], axis=1
            )
            lines = pl.ds(pl.multiple_of(block * cells_x, cells_x), cells_x)
            target = pl.ds(pl.multiple_of(block * count, count), count)
            for t in range(tracers):
                picked_x[t, target, :] = dot(at_i, kernel_x_ref[t, lines, :]).astype(BF16)

    pl.loop(0, 1)(pick_rows)
    by_x.wait_recv()
    by_y.wait_recv()
    from_x, from_y = profiles.at[:, 1 - i1, i2, i3], profiles.at[:, i1, 1 - i2, i3]
    diagonals = [
        send(from_x.at[:, 0 : half // 2], along),
        send(from_y.at[:, half // 2 : half], across),
    ]
    to_twin += [send(from_x, twin), send(from_y, twin)]
    pl.loop(1, 2)(pick_rows)
    for copy in diagonals:
        copy.wait_recv()
    to_twin.append(send(profiles.at[:, 1 - i1, 1 - i2, i3], twin))
    pl.loop(2, blocks // 2)(pick_rows)
    for copy in to_twin:
        copy.wait_recv()

    pieces = half // per_block
    acc[...] = jnp.zeros_like(acc)
    level = iota((layers, LANES), 0)
    lane_of = iota((layers, LANES), 1)

    @pl.loop(0, blocks // 2)
    def _(pair):
        for n in range(2):
            block = 2 * pair + n
            piece = pl.multiple_of(lax.rem(block, pieces) * per_block, per_block)
            part = profiles[:, :, :, :, pl.ds(piece, per_block), :].reshape(count, LANES)
            base = lax.div(block, pieces) * layers
            turned[n] = lax.dot_general(
                onehot(lane_of == level + base),
                part,
                (((1,), (1,)), ((), ())),
                preferred_element_type=F32,
            )
        lines = pl.ds(pl.multiple_of(pair * (2 * count), 2 * count), 2 * count)
        for t in range(tracers):
            for n in range(2):
                weights = smooth_y[2 * pair + n, t]
                for k in range(levels):
                    r = t * levels + k
                    value = jnp.broadcast_to(turned[n, r : r + 1, :], weights.shape).astype(BF16)
                    left[t, k * cells_y : (k + 1) * cells_y, n * count : (n + 1) * count] = (
                        weights * value
                    )
            acc[t] += dot(left[t], picked_x[t, lines, :])

    mask = mask_ref[...].astype(F32)
    carried = [None] * tracers
    for k in range(levels):
        lines = slice(k * cells_y, (k + 1) * cells_y)
        for t in range(tracers):
            value = acc[t, lines, :]
            if k > 0:
                value += coef_ref[k] * carried[t]
            carried[t] = value * inverse[k]
            acc[t, lines, :] = carried[t]
    for k in range(levels - 1, -1, -1):
        lines = slice(k * cells_y, (k + 1) * cells_y)
        for t in range(tracers):
            if k + 1 < levels:
                carried[t] = acc[t, lines, :] + ratio[k] * carried[t]
            inc_ref[t * levels + k] = (carried[t] * mask).astype(BF16)

    store = pltpu.make_async_copy(inc_ref, inc_hbm, store_sem.at[0])
    store.start()
    field = inc_ref[...].reshape(layers * cells_y, cells_x)
    found = dot(field, at_own).reshape(layers, cells_y, slots)
    in_row = iota((1, cells_y, slots), 1) == cell_j[None]
    picked = jnp.sum(jnp.where(in_row, found, 0.0), axis=1)
    picked = jnp.concatenate([picked, jnp.zeros((slots - layers, slots), F32)], axis=0).T
    for d in range(devices):
        outgoing[d] = picked[d * capacity : (d + 1) * capacity]
    arrived[me] = outgoing[me]

    for other, where in places:
        pltpu.make_async_remote_copy(
            src_ref=outgoing.at[other],
            dst_ref=arrived.at[me],
            send_sem=back_send,
            recv_sem=back_recv,
            device_id=where,
            device_id_type=MESH,
        ).start()
    for copy in sent:
        copy.wait_send()
    all_of(cells, cell_send).wait()
    all_of(arrived, back_recv).wait()
    for d in range(devices):
        rows[d * capacity : (d + 1) * capacity] = arrived[d]
    equiv_ref[...] = jnp.where(live, rows[...].T[:layers], 0.0).astype(BF16)
    result = pltpu.make_async_copy(equiv_ref, equiv_hbm, store_sem.at[1])
    result.start()

    all_of(outgoing, back_send).wait()
    store.wait()
    result.wait()


def body_gather(
    dims,
    innovations,
    station_columns,
    profile_counts,
    land_mask,
    vertical_coef,
    inverse_x,
    inverse_y,
):
    layers, slots = innovations.shape[1:]
    devices = profile_counts.shape[1]
    devices_y = dims[2] * dims[3]
    capacity = slots // devices
    cells_y, cells_x = land_mask.shape
    tracers = inverse_x.shape[0]
    levels = layers // tracers
    blocks = dims[0] * dims[1]
    count = devices * devices_y * capacity
    anywhere = pl.BlockSpec(memory_space=pl.ANY)
    operands = (
        innovations[0],
        station_columns,
        profile_counts,
        land_mask,
        vertical_coef,
        inverse_x,
        inverse_y,
    )
    n_profile = dims[0] - 1 + 8
    increment, equivalents = pl.pallas_call(
        functools.partial(profile_kernel, dims, capacity),
        out_shape=(
            jax.ShapeDtypeStruct((layers, cells_y, cells_x), BF16),
            jax.ShapeDtypeStruct((layers, slots), BF16),
        ),
        in_specs=[anywhere] * len(operands),
        out_specs=(anywhere, anywhere),
        scratch_shapes=[pltpu.VMEM(x.shape, x.dtype) for x in operands]
        + [
            pltpu.VMEM((devices, 1, slots), jnp.int32),
            pltpu.VMEM(dims + (slots // 2, LANES), BF16),
            pltpu.VMEM((blocks, count, LANES), jnp.int32),
            pltpu.VMEM((tracers, blocks * count, cells_x), BF16),
            pltpu.VMEM((blocks, tracers, cells_y, count), BF16),
            pltpu.VMEM((tracers, levels * cells_y, 2 * count), BF16),
            pltpu.VMEM((2, layers, count), F32),
            pltpu.VMEM((tracers, levels * cells_y, cells_x), F32),
            pltpu.VMEM((levels, cells_y, cells_x), F32),
            pltpu.VMEM((levels, cells_y, cells_x), F32),
            pltpu.VMEM((layers, cells_y, cells_x), BF16),
            pltpu.VMEM((devices, capacity, LANES), F32),
            pltpu.VMEM((devices, capacity, LANES), F32),
            pltpu.VMEM((slots, LANES), F32),
            pltpu.VMEM((layers, slots), BF16),
            pltpu.SemaphoreType.DMA((len(operands),)),
            pltpu.SemaphoreType.DMA((2,)),
            pltpu.SemaphoreType.DMA,
            pltpu.SemaphoreType.DMA,
            pltpu.SemaphoreType.DMA((n_profile,)),
            pltpu.SemaphoreType.DMA((n_profile,)),
            pltpu.SemaphoreType.DMA,
            pltpu.SemaphoreType.DMA,
        ],
        compiler_params=pltpu.CompilerParams(
            collective_id=0, has_side_effects=True, vmem_limit_bytes=VMEM_BYTES
        ),
        name="smooth_profiles",
    )(*operands)
    parts = 4
    increment, equivalents = pl.pallas_call(
        functools.partial(hand_over_kernel, parts),
        out_shape=(
            jax.ShapeDtypeStruct(increment.shape, BF16),
            jax.ShapeDtypeStruct(equivalents.shape, BF16),
        ),
        in_specs=[anywhere] * 2,
        out_specs=(anywhere, anywhere),
        scratch_shapes=[
            pltpu.VMEM(increment.shape, BF16),
            pltpu.VMEM(equivalents.shape, BF16),
            pltpu.SemaphoreType.DMA((2 * (parts + 1),)),
        ],
        compiler_params=pltpu.CompilerParams(vmem_limit_bytes=VMEM_BYTES),
        name="hand_over",
    )(increment, equivalents)
    return increment, equivalents[None]


def hand_over_kernel(parts, inc_ref, equiv_ref, inc_out, equiv_out, inc_held, equiv_held, sem):
    height = inc_ref.shape[0] // parts
    steps = [(equiv_ref, equiv_held, equiv_out)]
    for k in range(parts):
        lines = pl.ds(k * height, height)
        steps.append((inc_ref.at[lines], inc_held.at[lines], inc_out.at[lines]))
    n = len(steps)
    ins = [pltpu.make_async_copy(a, b, sem.at[k]) for k, (a, b, _) in enumerate(steps)]
    outs = [pltpu.make_async_copy(b, c, sem.at[n + k]) for k, (_, b, c) in enumerate(steps)]
    for copy in ins:
        copy.start()
    for first, second in zip(ins, outs):
        first.wait()
        second.start()
    for copy in outs:
        copy.wait()


def plan(devices_x, devices_y, innovations, land_mask, inverse_x, inverse_y):
    devices = devices_x * devices_y
    layers, slots = innovations.shape[1:]
    capacity = slots // devices
    cells_x = land_mask.shape[1] // devices_x
    fits = (
        slots == LANES
        and 2 * layers == LANES
        and capacity * devices_y == TILE
        and slots == devices * capacity
        and devices_x % 2 == 0
        and devices_y == 4
        and devices_x % 4 == 0
        and cells_x % LANES == 0
        and cells_x & (cells_x - 1) == 0
        and cells_x <= 32 * 256
        and inverse_y.shape[1] <= LANES
    )
    return (devices_x // 2, 2, devices_y // 2, 2) if fits else None


def solution(mesh):
    in_specs = (
        P(("gx", "gy"), None, None),
        P(("gx", "gy"), None),
        P(("gx", "gy"), None),
        P("gy", "gx"),
        P(None, "gy", "gx"),
        P(None, None, "gx"),
        P(),
    )
    out_specs = (P(None, "gy", "gx"), P(("gx", "gy"), None, None))

    def run(innovations, columns, counts, land_mask, coef, inverse_x, inverse_y):
        dims = plan(
            mesh.shape["gx"], mesh.shape["gy"], innovations, land_mask, inverse_x, inverse_y
        )
        body = body_exchange if dims is None else functools.partial(body_gather, dims)
        return jax.shard_map(
            body, mesh=mesh, in_specs=in_specs, out_specs=out_specs, check_vma=False
        )(innovations, columns, counts, land_mask, coef, inverse_x, inverse_y)

    return run
```

```python
import functools
import jax
import jax.numpy as jnp
from jax import lax
from jax.experimental import pallas as pl
from jax.experimental.pallas import tpu as pltpu
from jax.sharding import PartitionSpec as P

LEV = 32
LANES = 128
TILE = 16
VMEM_BYTES = 56 << 20
MESH = pl.DeviceIdType.MESH
F32 = jnp.float32
BF16 = jnp.bfloat16


def vertical_solve(rhs_field, coupling):
    levels = coupling.shape[0]
    zero_row = jnp.zeros_like(coupling[0])
    ratios = []
    partial_sol = []
    for level in range(levels):
        upper_coef = coupling[level + 1] if level + 1 < levels else zero_row
        diagonal = 1.0 + coupling[level] + upper_coef
        if level == 0:
            denominator = diagonal
            carried = rhs_field[:, 0]
        else:
            denominator = diagonal + coupling[level] * ratios[-1]
            carried = rhs_field[:, level] + coupling[level] * partial_sol[-1]
        ratios.append(-upper_coef / denominator)
        partial_sol.append(carried / denominator)
    solution = [partial_sol[-1]]
    for level in range(levels - 2, -1, -1):
        solution.append(partial_sol[level] - ratios[level] * solution[-1])
    return jnp.stack(solution[::-1], axis=1)


def body_exchange(
    innovations, station_columns, profile_counts, land_mask, vertical_coef, inverse_x, inverse_y
):
    layers = innovations.shape[1]
    devices_all = lax.axis_size(("gx", "gy"))
    devices_y = lax.axis_size("gy")
    capacity = innovations.shape[2] // devices_all
    slots = devices_all * capacity
    cells_y, cells_x = land_mask.shape
    cell_count = cells_y * cells_x
    tracers = inverse_x.shape[0]
    slot_index = lax.broadcasted_iota(jnp.int32, (devices_all, capacity), 1)
    live_flat = (slot_index < profile_counts[0][:, None]).reshape(slots)
    outgoing = jnp.where(live_flat[None, None, :], innovations, jnp.zeros((), jnp.bfloat16))
    arrived = lax.all_to_all(
        outgoing.reshape(layers, 1, devices_all, capacity),
        ("gx", "gy"),
        split_axis=2,
        concat_axis=1,
        tiled=True,
    )
    arrived = arrived.reshape(layers, slots)
    columns = station_columns[0]
    mask_flat = land_mask.reshape(cell_count)
    sea_slot = mask_flat[columns] > 0
    line_values = jnp.where(sea_slot[None, :], arrived, jnp.zeros((), jnp.bfloat16))
    line_columns = columns.reshape(1, slots)
    empty = jnp.zeros((tracers, layers // tracers, cells_y, cells_x), jnp.float32)
    values_piece = lax.all_gather(line_values, "gx", axis=1, tiled=True)
    columns_piece = lax.all_gather(line_columns, "gx", axis=1, tiled=True)
    sources = values_piece.shape[1] // slots

    def one_source(k, accum):
        block_values = lax.dynamic_slice_in_dim(values_piece, k * slots, slots, 1)
        block_columns = lax.dynamic_slice_in_dim(columns_piece, k * slots, slots, 1)[0]
        dense = (
            jnp.zeros((layers, cell_count), jnp.float32)
            .at[:, block_columns]
            .add(block_values.astype(jnp.float32))
        )
        dense = dense.astype(jnp.bfloat16).reshape(tracers, layers // tracers, cells_y, cells_x)
        source = k * slots // slots
        kernel_rows = lax.dynamic_slice_in_dim(inverse_x, source * cells_x, cells_x, 1)
        return accum + jnp.einsum(
            "tkjn,tnm->tkjm", dense, kernel_rows, preferred_element_type=jnp.float32
        )

    summed_x = lax.fori_loop(0, sources, one_source, empty)
    along_x = summed_x.astype(jnp.bfloat16).reshape(layers, cells_y, cells_x)
    rows_y = layers // devices_y
    tracer_y = lax.axis_index("gy") * rows_y // LEV
    matrix_y = lax.dynamic_index_in_dim(inverse_y, tracer_y, 0, keepdims=False)
    product = jnp.einsum(
        "rjc,jm->rmc",
        lax.all_to_all(along_x, "gy", split_axis=0, concat_axis=1, tiled=True),
        matrix_y,
        preferred_element_type=jnp.float32,
    ).astype(jnp.bfloat16)
    along_y = lax.all_to_all(product, "gy", split_axis=1, concat_axis=0, tiled=True)
    mask_field = mask_flat.astype(jnp.float32)
    column_field = along_y.astype(jnp.float32).reshape(2, LEV, cell_count)
    solved = vertical_solve(column_field, vertical_coef.reshape(LEV, cell_count))
    increment = (
        (solved * mask_field[None, None, :]).astype(jnp.bfloat16).reshape(layers, cells_y, cells_x)
    )
    picked = increment.reshape(layers, cell_count)[:, columns]
    returned = lax.all_to_all(
        picked.reshape(layers, 1, devices_all, capacity),
        ("gx", "gy"),
        split_axis=2,
        concat_axis=1,
        tiled=True,
    )
    returned = returned.reshape(1, layers, slots)
    equivalents = jnp.where(live_flat[None, None, :], returned, jnp.zeros((), jnp.bfloat16))
    return (increment, equivalents)


def iota(shape, dim):
    return lax.broadcasted_iota(jnp.int32, shape, dim)


def onehot(condition):
    return jnp.where(condition, 1.0, 0.0).astype(BF16)


def dot(a, b):
    return jnp.dot(a, b, preferred_element_type=F32)


def profile_kernel(
    dims,
    capacity,
    innov_hbm,
    columns_hbm,
    counts_hbm,
    mask_hbm,
    coef_hbm,
    kernel_x_hbm,
    kernel_y_hbm,
    inc_hbm,
    equiv_hbm,
    innov_ref,
    columns_ref,
    counts_ref,
    mask_ref,
    coef_ref,
    kernel_x_ref,
    kernel_y_ref,
    cells,
    profiles,
    place_x,
    picked_x,
    smooth_y,
    left,
    turned,
    acc,
    inverse,
    ratio,
    inc_ref,
    outgoing,
    arrived,
    rows,
    equiv_ref,
    load_sem,
    store_sem,
    cell_send,
    cell_recv,
    prof_send,
    prof_recv,
    back_send,
    back_recv,
):
    gx_outer, gx_inner, gy_outer, gy_inner = dims
    blocks, devices_y = gx_outer * gx_inner, gy_outer * gy_inner
    gx, gy = lax.axis_index("gx"), lax.axis_index("gy")
    i0, i1 = gx // gx_inner, lax.rem(gx, gx_inner)
    i2, i3 = gy // gy_inner, lax.rem(gy, gy_inner)
    me = gx * devices_y + gy
    layers, slots = innov_ref.shape
    devices = blocks * devices_y
    levels, cells_y, cells_x = coef_ref.shape
    tracers, rows_j, _ = kernel_y_ref.shape
    per_block = devices_y * capacity
    count = devices * per_block
    by_capacity, by_cells_x = capacity.bit_length() - 1, cells_x.bit_length() - 1

    loads = [
        pltpu.make_async_copy(source, target, load_sem.at[k])
        for k, (source, target) in enumerate(
            [
                (columns_hbm, columns_ref),
                (mask_hbm, mask_ref),
                (counts_hbm, counts_ref),
                (innov_hbm, innov_ref),
                (coef_hbm, coef_ref),
                (kernel_y_hbm, kernel_y_ref),
                (kernel_x_hbm, kernel_x_ref),
            ]
        )
    ]
    for load in loads:
        load.start()

    def place(k):
        other = lax.rem(me + k, devices)
        return other, (lax.div(other, devices_y), lax.rem(other, devices_y))

    barrier = pltpu.get_barrier_semaphore()

    places = [place(k) for k in range(1, devices)]
    for _, where in places:
        pl.semaphore_signal(barrier, inc=1, device_id=where, device_id_type=MESH)

    loads[0].wait()
    loads[1].wait()
    columns = columns_ref[...]
    cell_i, cell_j = columns & (cells_x - 1), columns >> by_cells_x
    at_own = onehot(iota((cells_x, slots), 0) == cell_i)
    masks = dot(mask_ref[...].astype(F32).astype(BF16), at_own)
    sea = jnp.sum(jnp.where(iota((cells_y, slots), 0) == cell_j, masks, 0.0), 0, keepdims=True)
    cells[me] = jnp.where(sea > 0.0, columns, -1)
    pl.semaphore_wait(barrier, devices - 1)

    for _, where in places:
        pltpu.make_async_remote_copy(
            src_ref=cells.at[me],
            dst_ref=cells.at[me],
            send_sem=cell_send,
            recv_sem=cell_recv,
            device_id=where,
            device_id_type=MESH,
        ).start()

    def all_of(ref, sem):
        others = ref.at[pl.ds(0, devices - 1)]
        return pltpu.make_async_copy(others, others, sem)

    loads[2].wait()
    loads[3].wait()
    counts = jnp.broadcast_to(counts_ref[...].astype(F32), (8, devices)).astype(BF16)
    lane_count = dot(
        counts, onehot(iota((devices, slots), 0) == iota((devices, slots), 1) >> by_capacity)
    )[0:1]
    live = (iota((1, slots), 1) & (capacity - 1)).astype(F32) < lane_count
    values = jnp.where(live, innov_ref[...].astype(F32), 0.0)
    half = slots // 2
    packed = jnp.concatenate([values, pltpu.roll(values, half, 1)], axis=0).T
    profiles[i0, i1, i2, i3] = packed[0:half].astype(BF16)

    sent = []

    def send(block, partner):
        copy = pltpu.make_async_remote_copy(
            src_ref=block,
            dst_ref=block,
            send_sem=prof_send.at[len(sent)],
            recv_sem=prof_recv.at[len(sent)],
            device_id=partner,
            device_id_type=MESH,
        )
        copy.start()
        sent.append(copy)
        return copy

    across = (i0 * gx_inner + (1 - i1), gy)
    along = (gx, (1 - i2) * gy_inner + i3)
    twin = (gx, i2 * gy_inner + (1 - i3))
    far = [
        send(
            profiles.at[i0, i1, i2, i3],
            (lax.rem(i0 + k, gx_outer) * gx_inner + i1, gy),
        )
        for k in range(1, gx_outer)
    ]

    loads[4].wait()
    last = None
    for k in range(levels):
        diagonal = 1.0 + coef_ref[k]
        if k + 1 < levels:
            diagonal += coef_ref[k + 1]
        if k > 0:
            diagonal -= coef_ref[k] * last
        inv = 1.0 / diagonal
        inverse[k] = inv
        if k + 1 < levels:
            last = coef_ref[k + 1] * inv
            ratio[k] = last

    for copy in far:
        copy.wait_recv()
    own_line = profiles.at[:, i1, i2, i3]
    by_x = send(own_line, across)
    by_y = send(own_line, along)
    to_twin = [send(own_line, twin)]

    all_of(cells, cell_recv).wait()

    loads[5].wait()
    loads[6].wait()
    own_rows = onehot(iota((cells_y, rows_j), 1) == gy * cells_y + iota((cells_y, rows_j), 0))
    own_y = [
        lax.dot_general(
            own_rows, kernel_y_ref[t], (((1,), (1,)), ((), ())), preferred_element_type=F32
        ).astype(BF16)
        for t in range(tracers)
    ]
    row, lane = iota((per_block, LANES), 0), iota((per_block, LANES), 1)
    owner = row >> by_capacity
    first_lane = lane - (row & (capacity - 1))
    row_lane = lane - owner * cells_y
    sender = iota((devices, 1, 1), 0) * capacity
    join = jnp.where(iota((2 * slots, LANES), 0) < slots, 32.0, 1.0).astype(BF16)

    @pl.loop(0, blocks // 2)
    def _(pair):
        for block in (2 * pair, 2 * pair + 1):
            tile = jnp.zeros((per_block, slots), jnp.int32)
            for b in range(devices_y):
                tile = jnp.where(owner == b, cells[block * devices_y + b], tile)
            own_lane = first_lane[None] == sender
            parts = [
                jnp.where(own_lane, part.astype(F32)[None], 0.0).reshape(count, slots).astype(BF16)
                for part in (tile >> 5, tile & 31)
            ]
            cell = dot(jnp.concatenate(parts, axis=1), join).astype(jnp.int32)
            place_x[block] = jnp.where(cell < 0, -1, cell & (cells_x - 1))
            cell_rows = (cell >> by_cells_x).reshape(devices, per_block, LANES)
            at_j = onehot(cell_rows == row_lane[None]).reshape(count, LANES)[:, :rows_j]
            for t in range(tracers):
                smooth_y[block, t] = lax.dot_general(
                    own_y[t], at_j, (((1,), (1,)), ((), ())), preferred_element_type=F32
                ).astype(BF16)

    def pick_rows(pair):
        lane_row = iota((1, LANES), 1)
        for block in (2 * pair, 2 * pair + 1):
            column = place_x[block]
            at_i = jnp.concatenate(
                [onehot(column == lane_row + start) for start in range(0, cells_x, LANES)], axis=1
            )
            lines = pl.ds(pl.multiple_of(block * cells_x, cells_x), cells_x)
            target = pl.ds(pl.multiple_of(block * count, count), count)
            for t in range(tracers):
                picked_x[t, target, :] = dot(at_i, kernel_x_ref[t, lines, :]).astype(BF16)

    pl.loop(0, 1)(pick_rows)
    by_x.wait_recv()
    by_y.wait_recv()
    from_x, from_y = profiles.at[:, 1 - i1, i2, i3], profiles.at[:, i1, 1 - i2, i3]
    diagonals = [
        send(from_x.at[:, 0 : half // 2], along),
        send(from_y.at[:, half // 2 : half], across),
    ]
    to_twin += [send(from_x, twin), send(from_y, twin)]
    pl.loop(1, 2)(pick_rows)
    for copy in diagonals:
        copy.wait_recv()
    to_twin.append(send(profiles.at[:, 1 - i1, 1 - i2, i3], twin))
    pl.loop(2, blocks // 2)(pick_rows)
    for copy in to_twin:
        copy.wait_recv()

    pieces = half // per_block
    acc[...] = jnp.zeros_like(acc)
    level = iota((layers, LANES), 0)
    lane_of = iota((layers, LANES), 1)

    @pl.loop(0, blocks // 4)
    def _(group):
        for n in range(4):
            block = 4 * group + n
            piece = pl.multiple_of(lax.rem(block, pieces) * per_block, per_block)
            part = profiles[:, :, :, :, pl.ds(piece, per_block), :].reshape(count, LANES)
            base = lax.div(block, pieces) * layers
            turned[n] = lax.dot_general(
                onehot(lane_of == level + base),
                part,
                (((1,), (1,)), ((), ())),
                preferred_element_type=F32,
            )
        lines = pl.ds(pl.multiple_of(group * (4 * count), 4 * count), 4 * count)
        for t in range(tracers):
            for n in range(4):
                weights = smooth_y[4 * group + n, t]
                for k in range(levels):
                    r = t * levels + k
                    value = jnp.broadcast_to(turned[n, r : r + 1, :], weights.shape).astype(BF16)
                    left[t, k * cells_y : (k + 1) * cells_y, n * count : (n + 1) * count] = (
                        weights * value
                    )
            acc[t] += dot(left[t], picked_x[t, lines, :])

    mask = mask_ref[...].astype(F32)
    carried = [None] * tracers
    for k in range(levels):
        lines = slice(k * cells_y, (k + 1) * cells_y)
        for t in range(tracers):
            value = acc[t, lines, :]
            if k > 0:
                value += coef_ref[k] * carried[t]
            carried[t] = value * inverse[k]
            acc[t, lines, :] = carried[t]
    for k in range(levels - 1, -1, -1):
        lines = slice(k * cells_y, (k + 1) * cells_y)
        for t in range(tracers):
            if k + 1 < levels:
                carried[t] = acc[t, lines, :] + ratio[k] * carried[t]
            inc_ref[t * levels + k] = (carried[t] * mask).astype(BF16)

    store = pltpu.make_async_copy(inc_ref, inc_hbm, store_sem.at[0])
    store.start()
    field = inc_ref[...].reshape(layers * cells_y, cells_x)
    found = dot(field, at_own).reshape(layers, cells_y, slots)
    in_row = iota((1, cells_y, slots), 1) == cell_j[None]
    picked = jnp.sum(jnp.where(in_row, found, 0.0), axis=1)
    picked = jnp.concatenate([picked, jnp.zeros((slots - layers, slots), F32)], axis=0).T
    for d in range(devices):
        outgoing[d] = picked[d * capacity : (d + 1) * capacity]
    arrived[me] = outgoing[me]

    for other, where in places:
        pltpu.make_async_remote_copy(
            src_ref=outgoing.at[other],
            dst_ref=arrived.at[me],
            send_sem=back_send,
            recv_sem=back_recv,
            device_id=where,
            device_id_type=MESH,
        ).start()
    for copy in sent:
        copy.wait_send()
    all_of(cells, cell_send).wait()
    all_of(arrived, back_recv).wait()
    for d in range(devices):
        rows[d * capacity : (d + 1) * capacity] = arrived[d]
    equiv_ref[...] = jnp.where(live, rows[...].T[:layers], 0.0).astype(BF16)
    result = pltpu.make_async_copy(equiv_ref, equiv_hbm, store_sem.at[1])
    result.start()

    all_of(outgoing, back_send).wait()
    store.wait()
    result.wait()


def body_gather(
    dims,
    innovations,
    station_columns,
    profile_counts,
    land_mask,
    vertical_coef,
    inverse_x,
    inverse_y,
):
    layers, slots = innovations.shape[1:]
    devices = profile_counts.shape[1]
    devices_y = dims[2] * dims[3]
    capacity = slots // devices
    cells_y, cells_x = land_mask.shape
    tracers = inverse_x.shape[0]
    levels = layers // tracers
    blocks = dims[0] * dims[1]
    count = devices * devices_y * capacity
    anywhere = pl.BlockSpec(memory_space=pl.ANY)
    operands = (
        innovations[0],
        station_columns,
        profile_counts,
        land_mask,
        vertical_coef,
        inverse_x,
        inverse_y,
    )
    n_profile = dims[0] - 1 + 8
    increment, equivalents = pl.pallas_call(
        functools.partial(profile_kernel, dims, capacity),
        out_shape=(
            jax.ShapeDtypeStruct((layers, cells_y, cells_x), BF16),
            jax.ShapeDtypeStruct((layers, slots), BF16),
        ),
        in_specs=[anywhere] * len(operands),
        out_specs=(anywhere, anywhere),
        scratch_shapes=[pltpu.VMEM(x.shape, x.dtype) for x in operands]
        + [
            pltpu.VMEM((devices, 1, slots), jnp.int32),
            pltpu.VMEM(dims + (slots // 2, LANES), BF16),
            pltpu.VMEM((blocks, count, LANES), jnp.int32),
            pltpu.VMEM((tracers, blocks * count, cells_x), BF16),
            pltpu.VMEM((blocks, tracers, cells_y, count), BF16),
            pltpu.VMEM((tracers, levels * cells_y, 4 * count), BF16),
            pltpu.VMEM((4, layers, count), F32),
            pltpu.VMEM((tracers, levels * cells_y, cells_x), F32),
            pltpu.VMEM((levels, cells_y, cells_x), F32),
            pltpu.VMEM((levels, cells_y, cells_x), F32),
            pltpu.VMEM((layers, cells_y, cells_x), BF16),
            pltpu.VMEM((devices, capacity, LANES), F32),
            pltpu.VMEM((devices, capacity, LANES), F32),
            pltpu.VMEM((slots, LANES), F32),
            pltpu.VMEM((layers, slots), BF16),
            pltpu.SemaphoreType.DMA((len(operands),)),
            pltpu.SemaphoreType.DMA((2,)),
            pltpu.SemaphoreType.DMA,
            pltpu.SemaphoreType.DMA,
            pltpu.SemaphoreType.DMA((n_profile,)),
            pltpu.SemaphoreType.DMA((n_profile,)),
            pltpu.SemaphoreType.DMA,
            pltpu.SemaphoreType.DMA,
        ],
        compiler_params=pltpu.CompilerParams(
            collective_id=0, has_side_effects=True, vmem_limit_bytes=VMEM_BYTES
        ),
        name="smooth_profiles",
    )(*operands)
    parts = 4
    increment, equivalents = pl.pallas_call(
        functools.partial(hand_over_kernel, parts),
        out_shape=(
            jax.ShapeDtypeStruct(increment.shape, BF16),
            jax.ShapeDtypeStruct(equivalents.shape, BF16),
        ),
        in_specs=[anywhere] * 2,
        out_specs=(anywhere, anywhere),
        scratch_shapes=[
            pltpu.VMEM(increment.shape, BF16),
            pltpu.VMEM(equivalents.shape, BF16),
            pltpu.SemaphoreType.DMA((2 * (parts + 1),)),
        ],
        compiler_params=pltpu.CompilerParams(vmem_limit_bytes=VMEM_BYTES),
        name="hand_over",
    )(increment, equivalents)
    return increment, equivalents[None]


def hand_over_kernel(parts, inc_ref, equiv_ref, inc_out, equiv_out, inc_held, equiv_held, sem):
    height = inc_ref.shape[0] // parts
    steps = [(equiv_ref, equiv_held, equiv_out)]
    for k in range(parts):
        lines = pl.ds(k * height, height)
        steps.append((inc_ref.at[lines], inc_held.at[lines], inc_out.at[lines]))
    n = len(steps)
    ins = [pltpu.make_async_copy(a, b, sem.at[k]) for k, (a, b, _) in enumerate(steps)]
    outs = [pltpu.make_async_copy(b, c, sem.at[n + k]) for k, (_, b, c) in enumerate(steps)]
    for copy in ins:
        copy.start()
    for first, second in zip(ins, outs):
        first.wait()
        second.start()
    for copy in outs:
        copy.wait()


def plan(devices_x, devices_y, innovations, land_mask, inverse_x, inverse_y):
    devices = devices_x * devices_y
    layers, slots = innovations.shape[1:]
    capacity = slots // devices
    cells_x = land_mask.shape[1] // devices_x
    fits = (
        slots == LANES
        and 2 * layers == LANES
        and capacity * devices_y == TILE
        and slots == devices * capacity
        and devices_x % 2 == 0
        and devices_y == 4
        and devices_x % 4 == 0
        and cells_x % LANES == 0
        and cells_x & (cells_x - 1) == 0
        and cells_x <= 32 * 256
        and inverse_y.shape[1] <= LANES
    )
    return (devices_x // 2, 2, devices_y // 2, 2) if fits else None


def solution(mesh):
    in_specs = (
        P(("gx", "gy"), None, None),
        P(("gx", "gy"), None),
        P(("gx", "gy"), None),
        P("gy", "gx"),
        P(None, "gy", "gx"),
        P(None, None, "gx"),
        P(),
    )
    out_specs = (P(None, "gy", "gx"), P(("gx", "gy"), None, None))

    def run(innovations, columns, counts, land_mask, coef, inverse_x, inverse_y):
        dims = plan(
            mesh.shape["gx"], mesh.shape["gy"], innovations, land_mask, inverse_x, inverse_y
        )
        body = body_exchange if dims is None else functools.partial(body_gather, dims)
        return jax.shard_map(
            body, mesh=mesh, in_specs=in_specs, out_specs=out_specs, check_vma=False
        )(innovations, columns, counts, land_mask, coef, inverse_x, inverse_y)

    return run
```
